32 devices in a mesh: gx: 4 (over y, x), gy: 2 (over core), gz: 4 (over z).
Axes of the slice: x: 2, y: 2, z: 4, core: 2. Of those that a mesh axis runs over, the one named last changes fastest.
Arguments:
- populations: float32 [19, 64, 32, 512], P(None, 'gz', 'gy', 'gx'), may hold values from 0.25 to 21, as said below
- solute_state: float32 [7, 256, 4096], P(None, ('gx', 'gy', 'gz')), may hold values from 0.05 to 3.9, as said below
- pore_mask: int32 [64, 32, 512], P('gz', 'gy', 'gx'), may hold values from 0 to 1, as said below
- block_slot: int32 [4, 2, 32], P('gz', 'gy', 'gx'), may hold values from -1 to 31, as said below
- slot_block: int32 [256], P(('gx', 'gy', 'gz')), may hold values from -1 to 31, as said below
Outputs:
- new_populations: float32 [19, 64, 32, 512], P(None, 'gz', 'gy', 'gx')
- new_solute: float32 [7, 256, 4096], P(None, ('gx', 'gy', 'gz'))
The draws below stay inside these ranges and needn't reach their ends.
Inputs may be any that keep to these rules, and one draw needn't show every extreme that they name: pore_mask is 1 only inside blocks listed in block_slot. `block_slot`: in each column of fixed gx and gy, the listed blocks are numbered k = 0, 1, ... in order of the gz index and then of the x block within the device; block k sits in owner k % 4 (index along gz within the same column), slot k // 4. Every device lists 1 to 8 blocks and in every column some device lists all 8, so one device hands 2 blocks to some owner. `slot_block`: the inverse of block_slot: an owner's filled slots come first, in increasing k. `populations`: Positive. `solute_state`: Positive.
All inputs are finite; a program needn't handle non-finite values.
Results may differ from the reference program's by a relative error of at most 0.0001.
Values sent between devices are 32-bit elements; how exact they have to be, the bound alone decides.
A program may use at most 192 MiB of HBM per device.

```python
import jax
import jax.numpy as jnp

BLOCK = 16
STEPS = 4
NBD = 8
OWN = 8
CELLS = 4096
NX = 512
NY = 32
NZ = 64
SLOTS = 256
N_GX = 4
N_GY = 2
N_GZ = 4


FLOW_WEIGHTS = [1.0 / 3.0] + [1.0 / 18.0] * 6 + [1.0 / 36.0] * 12


SOLUTE_WEIGHTS = [0.25] + [0.125] * 6


def layout(key):
    count_key, pick_key, full_key, voxel_key = jax.random.split(key, 4)
    counts = jax.random.randint(count_key, (N_GX, N_GY, N_GZ), 1, NBD + 1)
    fullest = jax.random.randint(full_key, (N_GX, N_GY), 0, N_GZ)
    counts = jnp.where(jnp.arange(N_GZ)[None, None, :] == fullest[:, :, None], NBD, counts)
    scores = jax.random.randint(pick_key, (N_GX, N_GY, N_GZ, NBD), 0, 1 << 20) * NBD + jnp.arange(NBD)[None, None, None, :]
    ranks = jnp.argsort(jnp.argsort(scores, axis=-1, stable=True), axis=-1, stable=True)
    flags = (ranks < counts[..., None]).astype(jnp.int32)
    flat_flags = flags.reshape(N_GX, N_GY, N_GZ * NBD)
    number = jnp.cumsum(flat_flags, axis=-1) - flat_flags
    owner_gz = number % N_GZ
    within = number // N_GZ
    slot_value = jnp.where(flat_flags > 0, owner_gz * OWN + within, -1)
    block_slot = slot_value.reshape(N_GX, N_GY, N_GZ, NBD).transpose(2, 1, 0, 3).reshape(N_GZ, N_GY, N_GX * NBD)
    position = jnp.broadcast_to(jnp.arange(N_GZ * NBD)[None, None, :], (N_GX, N_GY, N_GZ * NBD))
    target = jnp.where(flat_flags > 0, slot_value, N_GZ * OWN)
    column_x = jnp.broadcast_to(jnp.arange(N_GX)[:, None, None], target.shape)
    column_y = jnp.broadcast_to(jnp.arange(N_GY)[None, :, None], target.shape)
    slot_block = jnp.full((N_GX, N_GY, N_GZ * OWN), -1, jnp.int32)
    slot_block = slot_block.at[column_x, column_y, target].set(position.astype(jnp.int32), mode='drop')
    slot_block = slot_block.reshape(N_GX * N_GY * N_GZ * OWN)
    block_open = (block_slot >= 0).astype(jnp.int32)
    block_open = jnp.repeat(jnp.repeat(jnp.repeat(block_open, BLOCK, axis=0), BLOCK, axis=1), BLOCK, axis=2)
    voxels = (jax.random.randint(voxel_key, (NZ, NY, NX), 0, 100) < 27).astype(jnp.int32)
    return (block_open * voxels, block_slot.astype(jnp.int32), slot_block)


def draw_pore_mask(key, part):
    return layout(key)[0]


def draw_block_slot(key, part):
    return layout(key)[1]


def draw_slot_block(key, part):
    return layout(key)[2]


def draw_populations(key, part):
    key = jax.random.fold_in(key, 11)
    weights = jnp.array(FLOW_WEIGHTS, jnp.float32)[:, None, None, None]
    factor = jax.random.uniform(key, (19, NZ, NY, NX), jnp.float32, 0.5, 1.5)
    return weights * 36.0 * factor


def draw_solute_state(key, part):
    key = jax.random.fold_in(key, 23)
    weights = jnp.array(SOLUTE_WEIGHTS, jnp.float32)[:, None, None]
    factor = jax.random.uniform(key, (7, SLOTS, CELLS), jnp.float32, 0.2, 1.8)
    return weights * 8.0 * factor


def setup_inputs(seed: int = 0) -> dict:
    splits = jax.random.split(jax.random.key(seed), 6)
    populations = draw_populations(jax.random.fold_in(splits[5], 71), 0)
    solute_state = draw_solute_state(jax.random.fold_in(splits[5], 71), 0)
    pore_mask = draw_pore_mask(jax.random.fold_in(splits[5], 71), 0)
    block_slot = draw_block_slot(jax.random.fold_in(splits[5], 71), 0)
    slot_block = draw_slot_block(jax.random.fold_in(splits[5], 71), 0)
    return {"populations": populations, "solute_state": solute_state, "pore_mask": pore_mask, "block_slot": block_slot, "slot_block": slot_block}


FLOW_DIRS = [(0, 0, 0), (1, 0, 0), (-1, 0, 0), (0, 1, 0), (0, -1, 0), (0, 0, 1), (0, 0, -1),
             (1, 1, 0), (-1, -1, 0), (1, -1, 0), (-1, 1, 0), (1, 0, 1), (-1, 0, -1), (1, 0, -1),
             (-1, 0, 1), (0, 1, 1), (0, -1, -1), (0, 1, -1), (0, -1, 1)]
FLOW_WEIGHTS = [1.0 / 3.0] + [1.0 / 18.0] * 6 + [1.0 / 36.0] * 12
SOLUTE_DIRS = FLOW_DIRS[:7]
SOLUTE_WEIGHTS = [0.25] + [0.125] * 6
OMEGA_FLOW = 1.2
OMEGA_SOLUTE = 1.5
FORCE_GAIN = 0.02
REST_CONC = 8.0


def opposite(directions):
    return [directions.index((-a, -b, -c)) for (a, b, c) in directions]


def moments(populations, porous):
    density = jnp.sum(populations, axis=0)
    parts = []
    for coord in range(3):
        summed = jnp.zeros_like(density)
        for which, vector in enumerate(FLOW_DIRS):
            if vector[coord] != 0:
                summed = summed + vector[coord] * populations[which]
        parts.append(porous * summed / density)
    return density, jnp.stack(parts)


def solute_collide(solute, velocity):
    concentration = jnp.sum(solute, axis=0)
    results = []
    for which, vector in enumerate(SOLUTE_DIRS):
        along = vector[0] * velocity[0] + vector[1] * velocity[1] + vector[2] * velocity[2]
        balance = SOLUTE_WEIGHTS[which] * concentration * (1.0 + 4.0 * along)
        results.append(solute[which] + OMEGA_SOLUTE * (balance - solute[which]))
    return jnp.stack(results)


def flow_collide(populations, density, velocity, concentration, porous):
    uplift = porous * FORCE_GAIN * (concentration - REST_CONC)
    shift_x, shift_y, shift_z = velocity[0], velocity[1], velocity[2] + uplift
    square = shift_x * shift_x + shift_y * shift_y + shift_z * shift_z
    results = []
    for which, vector in enumerate(FLOW_DIRS):
        along = vector[0] * shift_x + vector[1] * shift_y + vector[2] * shift_z
        balance = FLOW_WEIGHTS[which] * density * (1.0 + 3.0 * along + 4.5 * along * along - 1.5 * square)
        relaxed = populations[which] + OMEGA_FLOW * (balance - populations[which])
        results.append(jnp.where(porous > 0, relaxed, populations[which]))
    return jnp.stack(results)


def stream(post, padded, porous, padded_pore, directions):
    reverse = opposite(directions)
    size_z, size_y, size_x = porous.shape
    results = []
    for which, (step_x, step_y, step_z) in enumerate(directions):
        source = padded[which, 1 - step_z:1 - step_z + size_z, 1 - step_y:1 - step_y + size_y,
                        1 - step_x:1 - step_x + size_x]
        source_open = padded_pore[1 - step_z:1 - step_z + size_z, 1 - step_y:1 - step_y + size_y,
                                  1 - step_x:1 - step_x + size_x]
        moved = jnp.where(source_open > 0, source, post[reverse[which]])
        results.append(jnp.where(porous > 0, moved, post[which]))
    return jnp.stack(results)


def reference(populations, solute_state, pore_mask, block_slot, slot_block):
    porous = pore_mask.astype(jnp.float32)
    blocks_z, blocks_y, blocks_x = block_slot.shape
    listed = block_slot >= 0
    owner_gz = block_slot // OWN
    within = block_slot % OWN
    column_x = (jnp.arange(blocks_x, dtype=jnp.int32) // NBD)[None, None, :]
    column_y = jnp.arange(blocks_y, dtype=jnp.int32)[None, :, None]
    global_slot = ((column_x * N_GY + column_y) * N_GZ + owner_gz) * OWN + within
    slot_index = jnp.where(listed, global_slot, 0).reshape(-1).astype(jnp.int32)
    tile_data = solute_state[:, slot_index, :] * listed.reshape(1, -1, 1).astype(jnp.float32)
    tile_data = tile_data.reshape(7, blocks_z, blocks_y, blocks_x, BLOCK, BLOCK, BLOCK)
    solute_dense = tile_data.transpose(0, 1, 4, 2, 5, 3, 6).reshape(
        7, blocks_z * BLOCK, blocks_y * BLOCK, blocks_x * BLOCK)
    padded_pore = jnp.pad(porous, 1)
    wide = ((0, 0), (1, 1), (1, 1), (1, 1))
    for repeat in range(STEPS):
        density, velocity = moments(populations, porous)
        post_solute = solute_collide(solute_dense, velocity)
        solute_dense = stream(post_solute, jnp.pad(post_solute, wide), porous, padded_pore, SOLUTE_DIRS)
        concentration = jnp.sum(solute_dense, axis=0)
        post_flow = flow_collide(populations, density, velocity, concentration, porous)
        populations = stream(post_flow, jnp.pad(post_flow, wide), porous, padded_pore, FLOW_DIRS)
    back_tiles = solute_dense.reshape(7, blocks_z, BLOCK, blocks_y, BLOCK, blocks_x, BLOCK)
    back_tiles = back_tiles.transpose(0, 1, 3, 5, 2, 4, 6).reshape(7, blocks_z * blocks_y * blocks_x, CELLS)
    slot_count = solute_state.shape[1]
    slot_ids = jnp.arange(slot_count, dtype=jnp.int32)
    column = slot_ids // (N_GZ * OWN)
    slot_cx = column // N_GY
    slot_cy = column % N_GY
    held = slot_block >= 0
    safe_block = jnp.where(held, slot_block, 0).astype(jnp.int32)
    block_z = safe_block // NBD
    block_x = slot_cx * NBD + safe_block % NBD
    flat_index = ((block_z * blocks_y + slot_cy) * blocks_x + block_x).astype(jnp.int32)
    picked = back_tiles[:, flat_index, :]
    new_solute = jnp.where(held[None, :, None], picked, jnp.float32(0.0))
    return populations, new_solute
```

```python
import functools

import jax
import jax.numpy as jnp
from jax import lax
from jax.experimental import pallas as pl
from jax.experimental.pallas import tpu as pltpu
from jax.sharding import PartitionSpec as P

STEPS = 4
AXES = ("gx", "gy", "gz")

FLOW_DIRS = [
    (0, 0, 0),
    (1, 0, 0),
    (-1, 0, 0),
    (0, 1, 0),
    (0, -1, 0),
    (0, 0, 1),
    (0, 0, -1),
    (1, 1, 0),
    (-1, -1, 0),
    (1, -1, 0),
    (-1, 1, 0),
    (1, 0, 1),
    (-1, 0, -1),
    (1, 0, -1),
    (-1, 0, 1),
    (0, 1, 1),
    (0, -1, -1),
    (0, 1, -1),
    (0, -1, 1),
]
FLOW_WEIGHTS = [1.0 / 3.0] + [1.0 / 18.0] * 6 + [1.0 / 36.0] * 12
OPP = [FLOW_DIRS.index((-a, -b, -c)) for a, b, c in FLOW_DIRS]
OMEGA_FLOW = 1.2
OMEGA_SOLUTE = 1.5
FORCE_GAIN = 0.02
REST_CONC = 8.0
SIGNS = (1, -1)

X_SIDE = [[FLOW_DIRS.index((s, b, c)) for b, c in ((0, 0), (1, 0), (-1, 0), (0, 1), (0, -1))] for s in SIGNS]
Y_SIDE = [[FLOW_DIRS.index((a, s, c)) for a, c in ((0, 0), (1, 0), (-1, 0), (0, 1), (0, -1))] for s in SIGNS]
Z_SIDE = [[FLOW_DIRS.index((a, b, s)) for a, b in ((0, 0), (1, 0), (-1, 0), (0, 1), (0, -1))] for s in SIGNS]
X_OFFS = [(0, 0), (1, 0), (-1, 0), (0, 1), (0, -1)]


def side(sign):
    return 0 if sign > 0 else 1


def iota(axis, shape=(16, 128)):
    return lax.broadcasted_iota(jnp.int32, shape, axis)


def swap_chunks(v):
    sub = iota(0, (8, 128))
    chunk = lax.shift_right_logical(iota(1, (8, 128)), 4)
    for k in (1, 2, 4):
        sbit = (sub & k) != 0
        if k == 4:
            both = pltpu.roll(pltpu.roll(v, 64, 1), 4, 0)
            v = jnp.where(((sub ^ chunk) & k) == 0, v, both)
        else:
            up = pltpu.roll(pltpu.roll(v, 16 * k, 1), 8 - k, 0)
            down = pltpu.roll(pltpu.roll(v, 128 - 16 * k, 1), k, 0)
            same = ((sub ^ chunk) & k) == 0
            v = jnp.where(same, v, jnp.where(sbit, down, up))
    return v


def kernel(
    sizes, cap, pop_ref, sol_ref, mask_ref, bs_ref, sb_ref, out_pop, out_sol,
    F, G, S, U, B, XM, YM, ZM, XH, YH, YE, ZH, XC, YC, SM, SH,
    T, stage, recv, stage2, recv2,
    f_send, f_recv, s_send, s_recv, a_send, a_recv, b_send, b_recv, own_sem,
):
    n_x, n_y, n_z = sizes
    me = tuple(lax.axis_index(a) for a in AXES)
    lane = iota(1)
    row = iota(0)
    size_z = mask_ref.shape[0]
    slots = sb_ref.shape[0]
    tiles = bs_ref.shape[2]
    comps = sol_ref.shape[0]

    def exists(off):
        ok = None
        for pos, n, o in zip(me, sizes, off):
            if o == 0:
                continue
            c = (pos + o < n) if o > 0 else (pos >= 1)
            ok = c if ok is None else jnp.logical_and(ok, c)
        return ok

    def dev(off):
        return {a: p + o for a, p, o in zip(AXES, me, off)}

    neighbours = [c for c in FLOW_DIRS[1:]]

    XH[0] = jnp.zeros_like(XH[0])
    YH[0] = jnp.zeros_like(YH[0])
    YE[0] = jnp.zeros_like(YE[0])
    ZH[0] = jnp.zeros_like(ZH[0])

    barrier = pltpu.get_barrier_semaphore()
    count = jnp.int32(n_z - 1)
    for off in neighbours:
        if off[0] == 0 and off[1] == 0:
            continue
        ok = exists(off)
        count = count + ok.astype(jnp.int32)

        @pl.when(ok)
        def _(off=off):
            pl.semaphore_signal(barrier, inc=1, device_id=dev(off), device_id_type=pl.DeviceIdType.MESH)

    for k in range(1, n_z):
        other = lax.rem(me[2] + k, n_z)
        pl.semaphore_signal(
            barrier, inc=1, device_id={"gx": me[0], "gy": me[1], "gz": other},
            device_id_type=pl.DeviceIdType.MESH)

    def routing(values, per):
        group = [lax.div(jnp.maximum(v, 0), jnp.int32(per)) for v in values]
        held = [(v >= 0).astype(jnp.int32) for v in values]
        rank = []
        for s in range(len(values)):
            r = jnp.int32(0)
            for e in range(s):
                r = r + jnp.where(group[e] == group[s], held[e], 0)
            rank.append(r)
        pick = []
        for g in range(n_z):
            for p in range(cap):
                at = jnp.int32(0)
                for s in range(len(values)):
                    hit = jnp.logical_and(group[s] == g, rank[s] == p)
                    at = at + jnp.where(hit, held[s] * s, 0)
                pick.append(at)
        where = [(group[s] * cap + rank[s] + 1) * held[s] - 1 for s in range(len(values))]
        return pick, where

    slot_pick, slot_where = routing([sb_ref[s] for s in range(slots)], tiles)
    tile_pick, tile_where = routing([bs_ref[0, 0, j] for j in range(tiles)], slots)
    rows = T.shape[1] // slots

    def blocks_of(c, n):
        return [T[c, k * rows:(k + 1) * rows, :] for k in range(n)]

    def pairs_of(buf, c):
        return [buf[q // cap, q % cap, c] for q in range(n_z * cap)]

    def choose(index, options):
        at = jnp.full(options[0].shape, index, jnp.int32)
        out = jnp.zeros_like(options[0])
        for k, v in enumerate(options):
            out = jnp.where(at == k, v, out)
        return out

    def gather(c, _):
        for r in range(rows):
            T[c, pl.ds(r, slots, stride=rows), :] = sol_ref[c, :, r * 128:(r + 1) * 128]
        for q in range(n_z * cap):
            stage[q // cap, q % cap, c] = choose(slot_pick[q], blocks_of(c, slots))
        return 0

    lax.fori_loop(0, comps, gather, 0)
    pl.semaphore_wait(barrier, count)

    def exchange_blocks(src, dst, send, rec, own):
        copies = []
        for k in range(1, n_z):
            other = lax.rem(me[2] + k, n_z)
            copies.append(pltpu.make_async_remote_copy(
                src_ref=src.at[other], dst_ref=dst.at[me[2]],
                send_sem=send.at[k], recv_sem=rec.at[k],
                device_id={"gx": me[0], "gy": me[1], "gz": other},
                device_id_type=pl.DeviceIdType.MESH))
        for c in copies:
            c.start()
        mine = pltpu.make_async_copy(src.at[me[2]], dst.at[me[2]], own)
        mine.start()
        return copies + [mine]

    moving = exchange_blocks(stage, recv, a_send, a_recv, own_sem.at[0])

    def flow_messages(slot):
        out = []
        for si, s in enumerate(SIGNS):
            for m, (oy, oz) in enumerate(X_OFFS):
                out.append(((s, oy, oz), XM.at[si], XH.at[slot, si, m]))
        for si, s in enumerate(SIGNS):
            out.append(((0, s, 0), YM.at[si], YH.at[slot, si]))
            for zi, z in enumerate(SIGNS):
                src = YM.at[si, 3 + zi, pl.ds(size_z - 8 if z > 0 else 0, 8)]
                out.append(((0, s, z), src, YE.at[slot, si, zi]))
        for si, s in enumerate(SIGNS):
            out.append(((0, 0, s), ZM.at[si], ZH.at[slot, si]))
        return out

    def solute_messages():
        out = []
        for ax in range(3):
            for si, s in enumerate(SIGNS):
                off = tuple(s if a == ax else 0 for a in range(3))
                out.append((off, SM.at[ax, si], SH.at[ax, si]))
        return out

    def exchange(messages, send, rec):
        copies = []
        for k, (off, src, dst) in enumerate(messages):
            copy = pltpu.make_async_remote_copy(
                src_ref=src, dst_ref=dst, send_sem=send.at[k], recv_sem=rec(k),
                device_id=dev(off), device_id_type=pl.DeviceIdType.MESH)
            copies.append(copy)

            @pl.when(exists(off))
            def _(copy=copy):
                copy.start()

        def finish():
            for (off, _, _), copy in zip(messages, copies):
                back = tuple(-o for o in off)

                @pl.when(exists(back))
                def _(copy=copy):
                    copy.wait_recv()
            for (off, _, _), copy in zip(messages, copies):
                @pl.when(exists(off))
                def _(copy=copy):
                    copy.wait_send()
        return finish

    def pack_x(z, planes, acc):
        new = []
        at_z = (lane & 15) == z
        for si, s in enumerate(SIGNS):
            w = None
            for j, v in enumerate(planes[si]):
                r = pltpu.roll(v, 16 * j + 1 if s > 0 else 16 * j, 1) if (s > 0 or j) else v
                w = r if w is None else jnp.where((lane >= 16 * j), r, w)
            new.append(jnp.where(at_z, pltpu.roll(w, z, 1), acc[si]))
        return tuple(new)

    def pack_flow(z, values, acc):
        for si, s in enumerate(SIGNS):
            e = 15 if s > 0 else 0
            for j, d in enumerate(Y_SIDE[si]):
                YM[si, j, pl.ds(z, 1), :] = values[d][e:e + 1, :]
        return pack_x(z, [[values[d] for d in X_SIDE[si]] for si in range(2)], acc)

    def finish_pack(acc):
        for si, s in enumerate(SIGNS):
            XM[si] = acc[si]
            for j, d in enumerate(Z_SIDE[si]):
                ZM[si, j] = F[d, size_z if s > 0 else 1]

    zero2 = (jnp.zeros((16, 128), jnp.float32),) * 2

    def flow_halo(slot):
        for si, s in enumerate(SIGNS):
            for j, d in enumerate(Z_SIDE[si]):
                F[d, 0 if s > 0 else size_z + 1] = ZH[slot, si, j]
            for zi, z in enumerate(SIGNS):
                base = YH[slot, si, 3 + zi]
                e = YE[slot, si, zi, 7:8, :] if z > 0 else YE[slot, si, zi, 0:1, :]
                edge = row == (15 if z > 0 else 0)
                YC[si, zi] = pltpu.roll(jnp.where(edge, jnp.broadcast_to(e, (16, 128)), base), 1 if z > 0 else 15, 0)
            base = XH[slot, si, 0]
            g1 = pltpu.roll(jnp.where(row == 15, XH[slot, si, 1], base), 1, 0)
            g2 = pltpu.roll(jnp.where(row == 0, XH[slot, si, 2], base), 15, 0)
            g3 = jnp.where(lane == 48, pltpu.roll(XH[slot, si, 3], 113, 1), pltpu.roll(base, 1, 1))
            g4 = jnp.where(lane == 79, pltpu.roll(XH[slot, si, 4], 15, 1), pltpu.roll(base, 127, 1))
            c = jnp.where(lane < 16, base, g1)
            c = jnp.where(lane < 32, c, g2)
            c = jnp.where(lane < 48, c, g3)
            XC[si] = jnp.where(lane < 64, c, g4)

    def shifted_flow(slot, z, xz):
        out = [None]
        for d in range(1, 19):
            cx, cy, cz = FLOW_DIRS[d]
            v = F[d, z + (1 - cz)]
            if cy:
                si = side(cy)
                j = Y_SIDE[si].index(d)
                if j < 3:
                    e = YH[slot, si, j, pl.ds(z, 1), :]
                else:
                    e = YC[si, j - 3, pl.ds(z, 1), :]
                v = jnp.where(row == (0 if cy > 0 else 15), jnp.broadcast_to(e, (16, 128)),
                              pltpu.roll(v, 1 if cy > 0 else 15, 0))
            if cx:
                si = side(cx)
                j = X_SIDE[si].index(d)
                if cx > 0:
                    h = pltpu.roll(xz[0], 128 - 16 * j, 1) if j else xz[0]
                    v = jnp.where(lane == 0, h, pltpu.roll(v, 1, 1))
                else:
                    h = pltpu.roll(xz[1], 127 - 16 * j, 1)
                    v = jnp.where(lane == 127, h, pltpu.roll(v, 127, 1))
            out.append(v)
        return out

    def x_planes(refs, z):
        back = lax.rem(128 - z, 128)
        return [pltpu.roll(r, back, 1) for r in refs]

    def moments(z, p, porous):
        density = p[0]
        for v in p[1:]:
            density = density + v
        inv = porous / density
        m = []
        for ax in range(3):
            total = None
            for d in range(1, 19):
                if FLOW_DIRS[d][ax] > 0:
                    diff = p[d] - p[OPP[d]]
                    total = diff if total is None else total + diff
            m.append(total * inv)
        U[0, z] = density
        for ax in range(3):
            U[1 + ax, z] = m[ax]

    def fill(z, acc):
        porous = mask_ref[z].astype(jnp.float32)
        for d in range(19):
            F[d, z + 1] = porous
        p = [pop_ref[d, z] for d in range(19)]
        for d in range(19):
            out_pop[d, z] = p[d]
        moments(z, p, porous)
        return pack_flow(z, [porous] * 19, acc)

    finish_pack(lax.fori_loop(0, size_z, fill, zero2))
    exchange(flow_messages(0), f_send, lambda k: f_recv.at[0, k])()
    flow_halo(0)

    def link_bits(z, _):
        xz = x_planes([XC[0], XC[1]], z)
        moved = shifted_flow(0, z, xz)
        pore = mask_ref[z] > 0
        bits = jnp.where(pore, 1, 0)
        for d in range(1, 19):
            bits = bits | jnp.where(jnp.logical_and(pore, moved[d] > 0.5), 1 << d, 0)
        B[z] = bits
        return 0

    lax.fori_loop(0, size_z, link_bits, 0)

    for c in moving:
        c.wait()

    def place(c, _):
        for j in range(tiles):
            T[c, j * rows:(j + 1) * rows, :] = choose(tile_where[j], pairs_of(recv, c))
        for r in range(rows):
            v = T[c, pl.ds(r, tiles, stride=rows), :]
            G[c, r // 2, (r % 2) * 8:(r % 2) * 8 + 8, :] = swap_chunks(v)
        return 0

    lax.fori_loop(0, comps, place, 0)

    def unplace(c, _):
        for r in range(rows):
            T[c, pl.ds(r, tiles, stride=rows), :] = swap_chunks(G[c, r // 2, (r % 2) * 8:(r % 2) * 8 + 8, :])
        for q in range(n_z * cap):
            stage2[q // cap, q % cap, c] = choose(tile_pick[q], blocks_of(c, tiles))
        return 0

    def collide_solute(z, acc):
        g = [G[i, z] for i in range(7)]
        u = [U[1 + a, z] for a in range(3)]
        conc = g[0]
        for v in g[1:]:
            conc = conc + v
        post = [g[0] * (1 - OMEGA_SOLUTE) + (OMEGA_SOLUTE * 0.25) * conc]
        cw = (OMEGA_SOLUTE * 0.125) * conc
        for i in range(1, 7):
            ax = (i - 1) // 2
            f = 1.0 + 4.0 * u[ax] if i % 2 else 1.0 - 4.0 * u[ax]
            post.append(g[i] * (1 - OMEGA_SOLUTE) + cw * f)
        for i in range(7):
            S[i, z + 1] = post[i]
        SM[1, 0, pl.ds(z, 1), :] = post[3][15:16, :]
        SM[1, 1, pl.ds(z, 1), :] = post[4][0:1, :]
        at_z = lane == z
        return (jnp.where(at_z, pltpu.roll(post[1], z + 1, 1), acc[0]),
                jnp.where(at_z, pltpu.roll(post[2], z, 1), acc[1]))

    def stream_solute_collide_flow(z, acc):
        bits = B[z]
        pore = (bits & 1) != 0
        xz = x_planes([SH[0, 0], SH[0, 1]], z)
        s = [S[i, z + 1] for i in range(7)]
        new = [s[0]]
        for i in range(1, 7):
            cx, cy, cz = FLOW_DIRS[i]
            if cx > 0:
                v = jnp.where(lane == 0, xz[0], pltpu.roll(s[i], 1, 1))
            elif cx < 0:
                v = jnp.where(lane == 127, pltpu.roll(xz[1], 127, 1), pltpu.roll(s[i], 127, 1))
            elif cy:
                e = SH[1, side(cy), pl.ds(z, 1), :]
                v = jnp.where(row == (0 if cy > 0 else 15), jnp.broadcast_to(e, (16, 128)),
                              pltpu.roll(s[i], 1 if cy > 0 else 15, 0))
            else:
                v = S[i, z + (1 - cz)]
            new.append(jnp.where((bits & (1 << i)) != 0, v, jnp.where(pore, s[OPP[i]], s[i])))
        conc = new[0]
        for v in new[1:]:
            conc = conc + v
        for i in range(7):
            G[i, z] = new[i]
        rho = U[0, z]
        ux = U[1, z]
        uy = U[2, z]
        uz = U[3, z] + jnp.where(pore, FORCE_GAIN * (conc - REST_CONC), 0.0)
        base = 1.0 - 1.5 * (ux * ux + uy * uy + uz * uz)
        p = [out_pop[d, z] for d in range(19)]
        post = [None] * 19
        post[0] = jnp.where(pore, p[0] * (1 - OMEGA_FLOW) + (OMEGA_FLOW / 3.0) * rho * base, p[0])
        w1 = (OMEGA_FLOW / 18.0) * rho
        w2 = (OMEGA_FLOW / 36.0) * rho
        for d in range(1, 19, 2):
            o = OPP[d]
            along = None
            for c, u in zip(FLOW_DIRS[d], (ux, uy, uz)):
                if c:
                    along = (u if c > 0 else -u) if along is None else (along + u if c > 0 else along - u)
            w = w1 if d < 7 else w2
            even = base + 4.5 * along * along
            odd = 3.0 * along
            post[d] = jnp.where(pore, p[d] * (1 - OMEGA_FLOW) + w * (even + odd), p[d])
            post[o] = jnp.where(pore, p[o] * (1 - OMEGA_FLOW) + w * (even - odd), p[o])
        for d in range(19):
            F[d, z + 1] = post[d]
        return pack_flow(z, post, acc)

    def stream_flow(slot):
        def body(z, _):
            bits = B[z]
            pore = (bits & 1) != 0
            xz = x_planes([XC[0], XC[1]], z)
            moved = shifted_flow(slot, z, xz)
            here = [F[d, z + 1] for d in range(19)]
            p = [here[0]]
            for d in range(1, 19):
                p.append(jnp.where((bits & (1 << d)) != 0, moved[d], jnp.where(pore, here[OPP[d]], here[d])))
            for d in range(19):
                out_pop[d, z] = p[d]
            moments(z, p, jnp.where(pore, 1.0, 0.0))
            return 0
        lax.fori_loop(0, size_z, body, 0)

    def step(t, last):
        slot = lax.rem(t + 1, 2)
        acc = lax.fori_loop(0, size_z, collide_solute, zero2)
        for si in range(2):
            SM[0, si] = acc[si]
            SM[2, si] = S[5 + si, size_z if si == 0 else 1]
        exchange(solute_messages(), s_send, lambda k: s_recv.at[k])()
        S[5, 0] = SH[2, 0]
        S[6, size_z + 1] = SH[2, 1]
        finish_pack(lax.fori_loop(0, size_z, stream_solute_collide_flow, zero2))
        done = exchange(flow_messages(slot), f_send, lambda k: f_recv.at[slot, k])
        back = None
        if last:
            lax.fori_loop(0, comps, unplace, 0)
            back = exchange_blocks(stage2, recv2, b_send, b_recv, own_sem.at[1])
        done()
        flow_halo(slot)
        stream_flow(slot)
        return back

    lax.fori_loop(0, STEPS - 1, lambda t, _: (step(t, False), 0)[1], 0)
    back = step(jnp.int32(STEPS - 1), True)
    for c in back:
        c.wait()

    def deliver(c, _):
        for s in range(slots):
            T[c, s * rows:(s + 1) * rows, :] = choose(slot_where[s], pairs_of(recv2, c))
        for r in range(rows):
            out_sol[c, :, r * 128:(r + 1) * 128] = T[c, pl.ds(r, slots, stride=rows), :]
        return 0

    lax.fori_loop(0, comps, deliver, 0)


def shards(sizes, populations, solute_state, pore_mask, block_slot, slot_block):
    n_z = sizes[2]
    tiles = block_slot.shape[2]
    cap = -(-tiles // n_z)
    comps, slots, cells = solute_state.shape
    rows = cells // 128
    sz, sy, sx = pore_mask.shape
    f32 = jnp.float32
    blocks = pltpu.VMEM((n_z, cap, comps, rows, 128), f32)
    dma = pltpu.SemaphoreType.DMA
    vmem = pl.BlockSpec(memory_space=pltpu.VMEM)
    smem = pl.BlockSpec(memory_space=pltpu.SMEM)
    return pl.pallas_call(
        functools.partial(kernel, sizes, cap),
        out_shape=(
            jax.ShapeDtypeStruct(populations.shape, f32),
            jax.ShapeDtypeStruct(solute_state.shape, f32),
        ),
        in_specs=[vmem, vmem, vmem, smem, smem],
        out_specs=(vmem, vmem),
        scratch_shapes=[
            pltpu.VMEM((19, sz + 2, sy, sx), f32),
            pltpu.VMEM((7, sz, sy, sx), f32),
            pltpu.VMEM((7, sz + 2, sy, sx), f32),
            pltpu.VMEM((4, sz, sy, sx), f32),
            pltpu.VMEM((sz, sy, sx), jnp.int32),
            pltpu.VMEM((2, 16, 128), f32),
            pltpu.VMEM((2, 5, 16, 128), f32),
            pltpu.VMEM((2, 5, 16, 128), f32),
            pltpu.VMEM((2, 2, 5, 16, 128), f32),
            pltpu.VMEM((2, 2, 5, 16, 128), f32),
            pltpu.VMEM((2, 2, 2, 8, 128), f32),
            pltpu.VMEM((2, 2, 5, 16, 128), f32),
            pltpu.VMEM((2, 16, 128), f32),
            pltpu.VMEM((2, 2, 16, 128), f32),
            pltpu.VMEM((3, 2, 16, 128), f32),
            pltpu.VMEM((3, 2, 16, 128), f32),
            pltpu.VMEM((comps, slots * rows, 128), f32),
            blocks, blocks, blocks, blocks,
            dma((18,)), dma((2, 18)), dma((6,)), dma((6,)),
            dma((n_z,)), dma((n_z,)), dma((n_z,)), dma((n_z,)), dma((2,)),
        ],
        compiler_params=pltpu.CompilerParams(
            collective_id=0, has_side_effects=True, vmem_limit_bytes=40 * 1024 * 1024),
    )(populations, solute_state, pore_mask, block_slot, slot_block)


def solution(mesh):
    sizes = tuple(mesh.shape[a] for a in AXES)
    in_specs = (
        P(None, "gz", "gy", "gx"),
        P(None, ("gx", "gy", "gz"), None),
        P("gz", "gy", "gx"),
        P("gz", "gy", "gx"),
        P(("gx", "gy", "gz")),
    )
    out_specs = (P(None, "gz", "gy", "gx"), P(None, ("gx", "gy", "gz"), None))
    return jax.shard_map(
        functools.partial(shards, sizes), mesh=mesh, in_specs=in_specs, out_specs=out_specs, check_vma=False)
```

```python
import functools

import jax
import jax.numpy as jnp
from jax import lax
from jax.experimental import pallas as pl
from jax.experimental.pallas import tpu as pltpu
from jax.sharding import PartitionSpec as P

STEPS = 4
AXES = ("gx", "gy", "gz")

FLOW_DIRS = [
    (0, 0, 0),
    (1, 0, 0),
    (-1, 0, 0),
    (0, 1, 0),
    (0, -1, 0),
    (0, 0, 1),
    (0, 0, -1),
    (1, 1, 0),
    (-1, -1, 0),
    (1, -1, 0),
    (-1, 1, 0),
    (1, 0, 1),
    (-1, 0, -1),
    (1, 0, -1),
    (-1, 0, 1),
    (0, 1, 1),
    (0, -1, -1),
    (0, 1, -1),
    (0, -1, 1),
]
FLOW_WEIGHTS = [1.0 / 3.0] + [1.0 / 18.0] * 6 + [1.0 / 36.0] * 12
OPP = [FLOW_DIRS.index((-a, -b, -c)) for a, b, c in FLOW_DIRS]
OMEGA_FLOW = 1.2
OMEGA_SOLUTE = 1.5
FORCE_GAIN = 0.02
REST_CONC = 8.0
SIGNS = (1, -1)

X_SIDE = [[FLOW_DIRS.index((s, b, c)) for b, c in ((0, 0), (1, 0), (-1, 0), (0, 1), (0, -1))] for s in SIGNS]
Y_SIDE = [[FLOW_DIRS.index((a, s, c)) for a, c in ((0, 0), (1, 0), (-1, 0), (0, 1), (0, -1))] for s in SIGNS]
Z_SIDE = [[FLOW_DIRS.index((a, b, s)) for a, b in ((0, 0), (1, 0), (-1, 0), (0, 1), (0, -1))] for s in SIGNS]
X_OFFS = [(0, 0), (1, 0), (-1, 0), (0, 1), (0, -1)]


def side(sign):
    return 0 if sign > 0 else 1


UNROLL = 4


def planes_loop(n, body, init):
    def group(g, acc):
        for k in range(UNROLL):
            acc = body(g * UNROLL + k, acc)
        return acc
    return lax.fori_loop(0, n // UNROLL, group, init)


def iota(axis, shape=(16, 128)):
    return lax.broadcasted_iota(jnp.int32, shape, axis)


def swap_chunks(v):
    sub = iota(0, (8, 128))
    chunk = lax.shift_right_logical(iota(1, (8, 128)), 4)
    for k in (1, 2, 4):
        sbit = (sub & k) != 0
        if k == 4:
            both = pltpu.roll(pltpu.roll(v, 64, 1), 4, 0)
            v = jnp.where(((sub ^ chunk) & k) == 0, v, both)
        else:
            up = pltpu.roll(pltpu.roll(v, 16 * k, 1), 8 - k, 0)
            down = pltpu.roll(pltpu.roll(v, 128 - 16 * k, 1), k, 0)
            same = ((sub ^ chunk) & k) == 0
            v = jnp.where(same, v, jnp.where(sbit, down, up))
    return v


def kernel(
    sizes, cap, pop_hbm, sol_hbm, mask_hbm, bs_ref, sb_ref, pop_out, sol_out,
    out_pop, sol_ref, mask_ref,
    F, G, S, U, B, XM, YM, ZM, XH, YH, YE, ZH, XC, YC, SM, SH,
    T, stage, recv, stage2, recv2,
    f_send, f_recv, s_send, s_recv, a_send, a_recv, b_send, b_recv, own_sem, io_sem,
):
    n_x, n_y, n_z = sizes
    loads = [
        pltpu.make_async_copy(src, dst, io_sem.at[k])
        for k, (src, dst) in enumerate(((sol_hbm, sol_ref), (mask_hbm, mask_ref), (pop_hbm, out_pop)))
    ]
    for load in loads:
        load.start()
    me = tuple(lax.axis_index(a) for a in AXES)
    lane = iota(1)
    row = iota(0)
    size_z = mask_ref.shape[0]
    slots = sb_ref.shape[0]
    tiles = bs_ref.shape[2]
    comps = sol_ref.shape[0]

    def exists(off):
        ok = None
        for pos, n, o in zip(me, sizes, off):
            if o == 0:
                continue
            c = (pos + o < n) if o > 0 else (pos >= 1)
            ok = c if ok is None else jnp.logical_and(ok, c)
        return ok

    def dev(off):
        return {a: p + o for a, p, o in zip(AXES, me, off)}

    neighbours = [c for c in FLOW_DIRS[1:]]

    XH[0] = jnp.zeros_like(XH[0])
    YH[0] = jnp.zeros_like(YH[0])
    YE[0] = jnp.zeros_like(YE[0])
    ZH[0] = jnp.zeros_like(ZH[0])

    barrier = pltpu.get_barrier_semaphore()
    count = jnp.int32(n_z - 1)
    for off in neighbours:
        if off[0] == 0 and off[1] == 0:
            continue
        ok = exists(off)
        count = count + ok.astype(jnp.int32)

        @pl.when(ok)
        def _(off=off):
            pl.semaphore_signal(barrier, inc=1, device_id=dev(off), device_id_type=pl.DeviceIdType.MESH)

    for k in range(1, n_z):
        other = lax.rem(me[2] + k, n_z)
        pl.semaphore_signal(
            barrier, inc=1, device_id={"gx": me[0], "gy": me[1], "gz": other},
            device_id_type=pl.DeviceIdType.MESH)

    def routing(values, per):
        group = [lax.div(jnp.maximum(v, 0), jnp.int32(per)) for v in values]
        held = [(v >= 0).astype(jnp.int32) for v in values]
        rank = []
        for s in range(len(values)):
            r = jnp.int32(0)
            for e in range(s):
                r = r + jnp.where(group[e] == group[s], held[e], 0)
            rank.append(r)
        pick = []
        for g in range(n_z):
            for p in range(cap):
                at = jnp.int32(0)
                for s in range(len(values)):
                    hit = jnp.logical_and(group[s] == g, rank[s] == p)
                    at = at + jnp.where(hit, held[s] * s, 0)
                pick.append(at)
        where = [(group[s] * cap + rank[s] + 1) * held[s] - 1 for s in range(len(values))]
        return pick, where

    slot_pick, slot_where = routing([sb_ref[s] for s in range(slots)], tiles)
    tile_pick, tile_where = routing([bs_ref[0, 0, j] for j in range(tiles)], slots)
    rows = T.shape[1] // slots

    def blocks_of(c, n):
        return [T[c, k * rows:(k + 1) * rows, :] for k in range(n)]

    def pairs_of(buf, c):
        return [buf[q // cap, q % cap, c] for q in range(n_z * cap)]

    def choose(index, options):
        at = jnp.full(options[0].shape, index, jnp.int32)
        out = jnp.zeros_like(options[0])
        for k, v in enumerate(options):
            out = jnp.where(at == k, v, out)
        return out

    def gather(c, _):
        for r in range(rows):
            T[c, pl.ds(r, slots, stride=rows), :] = sol_ref[c, :, r * 128:(r + 1) * 128]
        for q in range(n_z * cap):
            stage[q // cap, q % cap, c] = choose(slot_pick[q], blocks_of(c, slots))
        return 0

    loads[0].wait()
    lax.fori_loop(0, comps, gather, 0)
    pl.semaphore_wait(barrier, count)

    def exchange_blocks(src, dst, send, rec, own):
        copies = []
        for k in range(1, n_z):
            other = lax.rem(me[2] + k, n_z)
            copies.append(pltpu.make_async_remote_copy(
                src_ref=src.at[other], dst_ref=dst.at[me[2]],
                send_sem=send.at[k], recv_sem=rec.at[k],
                device_id={"gx": me[0], "gy": me[1], "gz": other},
                device_id_type=pl.DeviceIdType.MESH))
        for c in copies:
            c.start()
        mine = pltpu.make_async_copy(src.at[me[2]], dst.at[me[2]], own)
        mine.start()
        return copies + [mine]

    moving = exchange_blocks(stage, recv, a_send, a_recv, own_sem.at[0])

    def flow_messages(slot):
        out = []
        for si, s in enumerate(SIGNS):
            for m, (oy, oz) in enumerate(X_OFFS):
                out.append(((s, oy, oz), XM.at[si], XH.at[slot, si, m]))
        for si, s in enumerate(SIGNS):
            out.append(((0, s, 0), YM.at[si], YH.at[slot, si]))
            for zi, z in enumerate(SIGNS):
                src = YM.at[si, 3 + zi, pl.ds(size_z - 8 if z > 0 else 0, 8)]
                out.append(((0, s, z), src, YE.at[slot, si, zi]))
        for si, s in enumerate(SIGNS):
            out.append(((0, 0, s), ZM.at[si], ZH.at[slot, si]))
        return out

    def solute_messages():
        out = []
        for ax in range(3):
            for si, s in enumerate(SIGNS):
                off = tuple(s if a == ax else 0 for a in range(3))
                out.append((off, SM.at[ax, si], SH.at[ax, si]))
        return out

    def exchange(messages, send, rec):
        copies = []
        for k, (off, src, dst) in enumerate(messages):
            copy = pltpu.make_async_remote_copy(
                src_ref=src, dst_ref=dst, send_sem=send.at[k], recv_sem=rec(k),
                device_id=dev(off), device_id_type=pl.DeviceIdType.MESH)
            copies.append(copy)

            @pl.when(exists(off))
            def _(copy=copy):
                copy.start()

        def finish():
            for (off, _, _), copy in zip(messages, copies):
                back = tuple(-o for o in off)

                @pl.when(exists(back))
                def _(copy=copy):
                    copy.wait_recv()
            for (off, _, _), copy in zip(messages, copies):
                @pl.when(exists(off))
                def _(copy=copy):
                    copy.wait_send()
        return finish

    def pack_x(z, planes, acc):
        new = []
        at_z = (lane & 15) == z
        for si, s in enumerate(SIGNS):
            w = None
            for j, v in enumerate(planes[si]):
                r = pltpu.roll(v, z + (16 * j + 1 if s > 0 else 16 * j), 1)
                w = r if w is None else jnp.where((lane >= 16 * j), r, w)
            new.append(jnp.where(at_z, w, acc[si]))
        return tuple(new)

    def pack_flow(z, values, acc):
        for si, s in enumerate(SIGNS):
            e = 15 if s > 0 else 0
            for j, d in enumerate(Y_SIDE[si]):
                YM[si, j, pl.ds(z, 1), :] = values[d][e:e + 1, :]
        return pack_x(z, [[values[d] for d in X_SIDE[si]] for si in range(2)], acc)

    def finish_pack(acc):
        for si, s in enumerate(SIGNS):
            XM[si] = acc[si]
            for j, d in enumerate(Z_SIDE[si]):
                ZM[si, j] = F[d, size_z if s > 0 else 1]

    zero2 = (jnp.zeros((16, 128), jnp.float32),) * 2

    def flow_halo(slot):
        for si, s in enumerate(SIGNS):
            for j, d in enumerate(Z_SIDE[si]):
                F[d, 0 if s > 0 else size_z + 1] = ZH[slot, si, j]
            for zi, z in enumerate(SIGNS):
                base = YH[slot, si, 3 + zi]
                e = YE[slot, si, zi, 7:8, :] if z > 0 else YE[slot, si, zi, 0:1, :]
                edge = row == (15 if z > 0 else 0)
                YC[si, zi] = pltpu.roll(jnp.where(edge, jnp.broadcast_to(e, (16, 128)), base), 1 if z > 0 else 15, 0)
            base = XH[slot, si, 0]
            g1 = pltpu.roll(jnp.where(row == 15, XH[slot, si, 1], base), 1, 0)
            g2 = pltpu.roll(jnp.where(row == 0, XH[slot, si, 2], base), 15, 0)
            g3 = jnp.where(lane == 48, pltpu.roll(XH[slot, si, 3], 113, 1), pltpu.roll(base, 1, 1))
            g4 = jnp.where(lane == 79, pltpu.roll(XH[slot, si, 4], 15, 1), pltpu.roll(base, 127, 1))
            c = jnp.where(lane < 16, base, g1)
            c = jnp.where(lane < 32, c, g2)
            c = jnp.where(lane < 48, c, g3)
            XC[si] = jnp.where(lane < 64, c, g4)

    def shifted_flow(slot, z, xz):
        out = [None]
        for d in range(1, 19):
            cx, cy, cz = FLOW_DIRS[d]
            v = F[d, z + (1 - cz)]
            if cy:
                si = side(cy)
                j = Y_SIDE[si].index(d)
                if j < 3:
                    e = YH[slot, si, j, pl.ds(z, 1), :]
                else:
                    e = YC[si, j - 3, pl.ds(z, 1), :]
                v = jnp.where(row == (0 if cy > 0 else 15), jnp.broadcast_to(e, (16, 128)),
                              pltpu.roll(v, 1 if cy > 0 else 15, 0))
            if cx:
                si = side(cx)
                j = X_SIDE[si].index(d)
                if cx > 0:
                    h = pltpu.roll(xz[0], (128 - 16 * j) - z if j else lax.rem(128 - z, 128), 1)
                    v = jnp.where(lane == 0, h, pltpu.roll(v, 1, 1))
                else:
                    h = pltpu.roll(xz[1], (127 - 16 * j) - z, 1)
                    v = jnp.where(lane == 127, h, pltpu.roll(v, 127, 1))
            out.append(v)
        return out

    def moments(z, p, porous):
        density = p[0]
        for v in p[1:]:
            density = density + v
        inv = porous / density
        m = []
        for ax in range(3):
            total = None
            for d in range(1, 19):
                if FLOW_DIRS[d][ax] > 0:
                    diff = p[d] - p[OPP[d]]
                    total = diff if total is None else total + diff
            m.append(total * inv)
        U[0, z] = density
        for ax in range(3):
            U[1 + ax, z] = m[ax]

    loads[1].wait()
    loads[2].wait()

    def fill(z, acc):
        porous = mask_ref[z].astype(jnp.float32)
        for d in range(19):
            F[d, z + 1] = porous
        moments(z, [out_pop[d, z] for d in range(19)], porous)
        return pack_flow(z, [porous] * 19, acc)

    finish_pack(planes_loop(size_z, fill, zero2))
    exchange(flow_messages(0), f_send, lambda k: f_recv.at[0, k])()
    flow_halo(0)

    def link_bits(z, _):
        xz = [XC[0], XC[1]]
        moved = shifted_flow(0, z, xz)
        pore = mask_ref[z] > 0
        bits = jnp.where(pore, 1, 0)
        for d in range(1, 19):
            bits = bits | jnp.where(jnp.logical_and(pore, moved[d] > 0.5), 1 << d, 0)
        B[z] = bits
        return 0

    planes_loop(size_z, link_bits, 0)

    for c in moving:
        c.wait()

    def place(c, _):
        for j in range(tiles):
            T[c, j * rows:(j + 1) * rows, :] = choose(tile_where[j], pairs_of(recv, c))
        for r in range(rows):
            v = T[c, pl.ds(r, tiles, stride=rows), :]
            G[c, r // 2, (r % 2) * 8:(r % 2) * 8 + 8, :] = swap_chunks(v)
        return 0

    lax.fori_loop(0, comps, place, 0)

    def unplace(c, _):
        for r in range(rows):
            T[c, pl.ds(r, tiles, stride=rows), :] = swap_chunks(G[c, r // 2, (r % 2) * 8:(r % 2) * 8 + 8, :])
        for q in range(n_z * cap):
            stage2[q // cap, q % cap, c] = choose(tile_pick[q], blocks_of(c, tiles))
        return 0

    def collide_solute(z, acc):
        g = [G[i, z] for i in range(7)]
        u = [U[1 + a, z] for a in range(3)]
        conc = g[0]
        for v in g[1:]:
            conc = conc + v
        post = [g[0] * (1 - OMEGA_SOLUTE) + (OMEGA_SOLUTE * 0.25) * conc]
        cw = (OMEGA_SOLUTE * 0.125) * conc
        for i in range(1, 7):
            ax = (i - 1) // 2
            f = 1.0 + 4.0 * u[ax] if i % 2 else 1.0 - 4.0 * u[ax]
            post.append(g[i] * (1 - OMEGA_SOLUTE) + cw * f)
        for i in range(7):
            S[i, z + 1] = post[i]
        SM[1, 0, pl.ds(z, 1), :] = post[3][15:16, :]
        SM[1, 1, pl.ds(z, 1), :] = post[4][0:1, :]
        at_z = lane == z
        return (jnp.where(at_z, pltpu.roll(post[1], z + 1, 1), acc[0]),
                jnp.where(at_z, pltpu.roll(post[2], z, 1), acc[1]))

    def stream_solute_collide_flow(z, acc):
        bits = B[z]
        pore = (bits & 1) != 0
        xz = [SH[0, 0], SH[0, 1]]
        s = [S[i, z + 1] for i in range(7)]
        new = [s[0]]
        for i in range(1, 7):
            cx, cy, cz = FLOW_DIRS[i]
            if cx > 0:
                v = jnp.where(lane == 0, pltpu.roll(xz[0], lax.rem(128 - z, 128), 1), pltpu.roll(s[i], 1, 1))
            elif cx < 0:
                v = jnp.where(lane == 127, pltpu.roll(xz[1], 127 - z, 1), pltpu.roll(s[i], 127, 1))
            elif cy:
                e = SH[1, side(cy), pl.ds(z, 1), :]
                v = jnp.where(row == (0 if cy > 0 else 15), jnp.broadcast_to(e, (16, 128)),
                              pltpu.roll(s[i], 1 if cy > 0 else 15, 0))
            else:
                v = S[i, z + (1 - cz)]
            new.append(jnp.where((bits & (1 << i)) != 0, v, jnp.where(pore, s[OPP[i]], s[i])))
        conc = new[0]
        for v in new[1:]:
            conc = conc + v
        for i in range(7):
            G[i, z] = new[i]
        rho = U[0, z]
        ux = U[1, z]
        uy = U[2, z]
        uz = U[3, z] + jnp.where(pore, FORCE_GAIN * (conc - REST_CONC), 0.0)
        base = 1.0 - 1.5 * (ux * ux + uy * uy + uz * uz)
        p = [out_pop[d, z] for d in range(19)]
        post = [None] * 19
        post[0] = jnp.where(pore, p[0] * (1 - OMEGA_FLOW) + (OMEGA_FLOW / 3.0) * rho * base, p[0])
        w1 = (OMEGA_FLOW / 18.0) * rho
        w2 = (OMEGA_FLOW / 36.0) * rho
        for d in range(1, 19, 2):
            o = OPP[d]
            along = None
            for c, u in zip(FLOW_DIRS[d], (ux, uy, uz)):
                if c:
                    along = (u if c > 0 else -u) if along is None else (along + u if c > 0 else along - u)
            w = w1 if d < 7 else w2
            even = base + 4.5 * along * along
            odd = 3.0 * along
            post[d] = jnp.where(pore, p[d] * (1 - OMEGA_FLOW) + w * (even + odd), p[d])
            post[o] = jnp.where(pore, p[o] * (1 - OMEGA_FLOW) + w * (even - odd), p[o])
        for d in range(19):
            F[d, z + 1] = post[d]
        return pack_flow(z, post, acc)

    def stream_flow(slot):
        def body(z, _):
            bits = B[z]
            pore = (bits & 1) != 0
            xz = [XC[0], XC[1]]
            moved = shifted_flow(slot, z, xz)
            here = [F[d, z + 1] for d in range(19)]
            p = [here[0]]
            for d in range(1, 19):
                p.append(jnp.where((bits & (1 << d)) != 0, moved[d], jnp.where(pore, here[OPP[d]], here[d])))
            for d in range(19):
                out_pop[d, z] = p[d]
            moments(z, p, jnp.where(pore, 1.0, 0.0))
            return 0
        planes_loop(size_z, body, 0)

    def step(t, last):
        slot = lax.rem(t + 1, 2)
        acc = planes_loop(size_z, collide_solute, zero2)
        for si in range(2):
            SM[0, si] = acc[si]
            SM[2, si] = S[5 + si, size_z if si == 0 else 1]
        exchange(solute_messages(), s_send, lambda k: s_recv.at[k])()
        S[5, 0] = SH[2, 0]
        S[6, size_z + 1] = SH[2, 1]
        finish_pack(planes_loop(size_z, stream_solute_collide_flow, zero2))
        done = exchange(flow_messages(slot), f_send, lambda k: f_recv.at[slot, k])
        back = None
        if last:
            lax.fori_loop(0, comps, unplace, 0)
            back = exchange_blocks(stage2, recv2, b_send, b_recv, own_sem.at[1])
        done()
        flow_halo(slot)
        stream_flow(slot)
        return back

    lax.fori_loop(0, STEPS - 1, lambda t, _: (step(t, False), 0)[1], 0)
    back = step(jnp.int32(STEPS - 1), True)
    store_pop = pltpu.make_async_copy(out_pop, pop_out, io_sem.at[3])
    store_pop.start()
    for c in back:
        c.wait()

    def deliver(c, _):
        for s in range(slots):
            T[c, s * rows:(s + 1) * rows, :] = choose(slot_where[s], pairs_of(recv2, c))
        for r in range(rows):
            sol_ref[c, :, r * 128:(r + 1) * 128] = T[c, pl.ds(r, slots, stride=rows), :]
        return 0

    lax.fori_loop(0, comps, deliver, 0)
    store_sol = pltpu.make_async_copy(sol_ref, sol_out, io_sem.at[4])
    store_sol.start()
    store_pop.wait()
    store_sol.wait()


def shards(sizes, populations, solute_state, pore_mask, block_slot, slot_block):
    n_z = sizes[2]
    tiles = block_slot.shape[2]
    cap = -(-tiles // n_z)
    comps, slots, cells = solute_state.shape
    rows = cells // 128
    sz, sy, sx = pore_mask.shape
    f32 = jnp.float32
    blocks = pltpu.VMEM((n_z, cap, comps, rows, 128), f32)
    dma = pltpu.SemaphoreType.DMA
    hbm = pl.BlockSpec(memory_space=pl.ANY)
    smem = pl.BlockSpec(memory_space=pltpu.SMEM)
    return pl.pallas_call(
        functools.partial(kernel, sizes, cap),
        out_shape=(
            jax.ShapeDtypeStruct(populations.shape, f32),
            jax.ShapeDtypeStruct(solute_state.shape, f32),
        ),
        in_specs=[hbm, hbm, hbm, smem, smem],
        out_specs=(hbm, hbm),
        scratch_shapes=[
            pltpu.VMEM(populations.shape, f32),
            pltpu.VMEM(solute_state.shape, f32),
            pltpu.VMEM(pore_mask.shape, jnp.int32),
            pltpu.VMEM((19, sz + 2, sy, sx), f32),
            pltpu.VMEM((7, sz, sy, sx), f32),
            pltpu.VMEM((7, sz + 2, sy, sx), f32),
            pltpu.VMEM((4, sz, sy, sx), f32),
            pltpu.VMEM((sz, sy, sx), jnp.int32),
            pltpu.VMEM((2, 16, 128), f32),
            pltpu.VMEM((2, 5, 16, 128), f32),
            pltpu.VMEM((2, 5, 16, 128), f32),
            pltpu.VMEM((2, 2, 5, 16, 128), f32),
            pltpu.VMEM((2, 2, 5, 16, 128), f32),
            pltpu.VMEM((2, 2, 2, 8, 128), f32),
            pltpu.VMEM((2, 2, 5, 16, 128), f32),
            pltpu.VMEM((2, 16, 128), f32),
            pltpu.VMEM((2, 2, 16, 128), f32),
            pltpu.VMEM((3, 2, 16, 128), f32),
            pltpu.VMEM((3, 2, 16, 128), f32),
            pltpu.VMEM((comps, slots * rows, 128), f32),
            blocks, blocks, blocks, blocks,
            dma((18,)), dma((2, 18)), dma((6,)), dma((6,)),
            dma((n_z,)), dma((n_z,)), dma((n_z,)), dma((n_z,)), dma((2,)), dma((5,)),
        ],
        compiler_params=pltpu.CompilerParams(
            collective_id=0, has_side_effects=True, vmem_limit_bytes=56 * 1024 * 1024),
    )(populations, solute_state, pore_mask, block_slot, slot_block)


def solution(mesh):
    sizes = tuple(mesh.shape[a] for a in AXES)
    in_specs = (
        P(None, "gz", "gy", "gx"),
        P(None, ("gx", "gy", "gz"), None),
        P("gz", "gy", "gx"),
        P("gz", "gy", "gx"),
        P(("gx", "gy", "gz")),
    )
    out_specs = (P(None, "gz", "gy", "gx"), P(None, ("gx", "gy", "gz"), None))
    return jax.shard_map(
        functools.partial(shards, sizes), mesh=mesh, in_specs=in_specs, out_specs=out_specs, check_vma=False)
```

```python
import functools

import jax
import jax.numpy as jnp
from jax import lax
from jax.experimental import pallas as pl
from jax.experimental.pallas import tpu as pltpu
from jax.sharding import PartitionSpec as P

STEPS = 4
AXES = ("gx", "gy", "gz")

FLOW_DIRS = [
    (0, 0, 0),
    (1, 0, 0),
    (-1, 0, 0),
    (0, 1, 0),
    (0, -1, 0),
    (0, 0, 1),
    (0, 0, -1),
    (1, 1, 0),
    (-1, -1, 0),
    (1, -1, 0),
    (-1, 1, 0),
    (1, 0, 1),
    (-1, 0, -1),
    (1, 0, -1),
    (-1, 0, 1),
    (0, 1, 1),
    (0, -1, -1),
    (0, 1, -1),
    (0, -1, 1),
]
FLOW_WEIGHTS = [1.0 / 3.0] + [1.0 / 18.0] * 6 + [1.0 / 36.0] * 12
OPP = [FLOW_DIRS.index((-a, -b, -c)) for a, b, c in FLOW_DIRS]
OMEGA_FLOW = 1.2
OMEGA_SOLUTE = 1.5
FORCE_GAIN = 0.02
REST_CONC = 8.0
SIGNS = (1, -1)

X_SIDE = [[FLOW_DIRS.index((s, b, c)) for b, c in ((0, 0), (1, 0), (-1, 0), (0, 1), (0, -1))] for s in SIGNS]
Y_SIDE = [[FLOW_DIRS.index((a, s, c)) for a, c in ((0, 0), (1, 0), (-1, 0), (0, 1), (0, -1))] for s in SIGNS]
Z_SIDE = [[FLOW_DIRS.index((a, b, s)) for a, b in ((0, 0), (1, 0), (-1, 0), (0, 1), (0, -1))] for s in SIGNS]
X_OFFS = [(0, 0), (1, 0), (-1, 0), (0, 1), (0, -1)]


def side(sign):
    return 0 if sign > 0 else 1


def planes_loop(n, body, init, first=0, unroll=4):
    def group(g, acc):
        for k in range(unroll):
            acc = body(first + g * unroll + k, acc)
        return acc
    return lax.fori_loop(0, n // unroll, group, init)


def iota(axis, shape=(16, 128)):
    return lax.broadcasted_iota(jnp.int32, shape, axis)


def swap_chunks(v):
    sub = iota(0, (8, 128))
    chunk = lax.shift_right_logical(iota(1, (8, 128)), 4)
    for k in (1, 2, 4):
        sbit = (sub & k) != 0
        if k == 4:
            both = pltpu.roll(pltpu.roll(v, 64, 1), 4, 0)
            v = jnp.where(((sub ^ chunk) & k) == 0, v, both)
        else:
            up = pltpu.roll(pltpu.roll(v, 16 * k, 1), 8 - k, 0)
            down = pltpu.roll(pltpu.roll(v, 128 - 16 * k, 1), k, 0)
            same = ((sub ^ chunk) & k) == 0
            v = jnp.where(same, v, jnp.where(sbit, down, up))
    return v


def kernel(
    sizes, cap, pop_hbm, sol_hbm, mask_hbm, bs_hbm, sb_hbm, out_pop, out_sol,
    sol_ref, mask_ref, bs_ref, sb_ref,
    F, G, S, U, B, XM, YM, ZM, XH, YH, YE, ZH, XC, YC, SM, SH,
    T, stage, recv, stage2, recv2,
    f_send, f_recv, s_send, s_recv, a_send, a_recv, b_send, b_recv, own_a, own_b, io_sem,
):
    n_x, n_y, n_z = sizes
    loads = [
        pltpu.make_async_copy(src, dst, io_sem.at[k])
        for k, (src, dst) in enumerate((
            (sb_hbm, sb_ref), (bs_hbm, bs_ref), (sol_hbm, sol_ref), (mask_hbm, mask_ref), (pop_hbm, out_pop)))
    ]
    for load in loads:
        load.start()
    me = tuple(lax.axis_index(a) for a in AXES)
    lane = iota(1)
    row = iota(0)
    size_z = mask_ref.shape[0]
    slots = sb_ref.shape[0]
    tiles = bs_ref.shape[2]
    comps = sol_ref.shape[0]

    def exists(off):
        ok = None
        for pos, n, o in zip(me, sizes, off):
            if o == 0:
                continue
            c = (pos + o < n) if o > 0 else (pos >= 1)
            ok = c if ok is None else jnp.logical_and(ok, c)
        return ok

    def dev(off):
        return {a: p + o for a, p, o in zip(AXES, me, off)}

    neighbours = [c for c in FLOW_DIRS[1:]]

    XH[0] = jnp.zeros_like(XH[0])
    YH[0] = jnp.zeros_like(YH[0])
    YE[0] = jnp.zeros_like(YE[0])
    ZH[0] = jnp.zeros_like(ZH[0])

    barrier = pltpu.get_barrier_semaphore()
    count = jnp.int32(n_z - 1)
    for off in neighbours:
        if off[0] == 0 and off[1] == 0:
            continue
        ok = exists(off)
        count = count + ok.astype(jnp.int32)

        @pl.when(ok)
        def _(off=off):
            pl.semaphore_signal(barrier, inc=1, device_id=dev(off), device_id_type=pl.DeviceIdType.MESH)

    for k in range(1, n_z):
        other = lax.rem(me[2] + k, n_z)
        pl.semaphore_signal(
            barrier, inc=1, device_id={"gx": me[0], "gy": me[1], "gz": other},
            device_id_type=pl.DeviceIdType.MESH)

    def routing(values, per):
        group = [lax.div(jnp.maximum(v, 0), jnp.int32(per)) for v in values]
        held = [(v >= 0).astype(jnp.int32) for v in values]
        rank = []
        for s in range(len(values)):
            r = jnp.int32(0)
            for e in range(s):
                r = r + jnp.where(group[e] == group[s], held[e], 0)
            rank.append(r)
        pick = []
        for g in range(n_z):
            for p in range(cap):
                at = jnp.int32(0)
                for s in range(len(values)):
                    hit = jnp.logical_and(group[s] == g, rank[s] == p)
                    at = at + jnp.where(hit, held[s] * s, 0)
                pick.append(at)
        where = [(group[s] * cap + rank[s] + 1) * held[s] - 1 for s in range(len(values))]
        return pick, where

    loads[0].wait()
    loads[1].wait()
    slot_pick, slot_where = routing([sb_ref[s] for s in range(slots)], tiles)
    tile_pick, tile_where = routing([bs_ref[0, 0, j] for j in range(tiles)], slots)
    rows = T.shape[1] // slots

    def blocks_of(c, n):
        return [T[c, k * rows:(k + 1) * rows, :] for k in range(n)]

    def pairs_of(buf, c):
        return [buf[c, q // cap, q % cap] for q in range(n_z * cap)]

    def choose(index, options):
        at = jnp.full(options[0].shape, index, jnp.int32)
        out = jnp.zeros_like(options[0])
        for k, v in enumerate(options):
            out = jnp.where(at == k, v, out)
        return out

    def gather(c, _):
        for r in range(rows):
            T[c, pl.ds(r, slots, stride=rows), :] = sol_ref[c, :, r * 128:(r + 1) * 128]
        for q in range(n_z * cap):
            stage[c, q // cap, q % cap] = choose(slot_pick[q], blocks_of(c, slots))
        return 0

    loads[2].wait()
    lax.fori_loop(0, comps, gather, 0)
    pl.semaphore_wait(barrier, count)

    hops = sorted(range(1, n_z), key=lambda k: abs(2 * k - n_z))

    def block_copies(c, src, dst, send, rec, own):
        copies = []
        for k in hops:
            other = lax.rem(me[2] + k, n_z)
            copies.append(pltpu.make_async_remote_copy(
                src_ref=src.at[c, other], dst_ref=dst.at[c, me[2]],
                send_sem=send.at[k, c], recv_sem=rec.at[k, c],
                device_id={"gx": me[0], "gy": me[1], "gz": other},
                device_id_type=pl.DeviceIdType.MESH))
        copies.append(pltpu.make_async_copy(src.at[c, me[2]], dst.at[c, me[2]], own.at[c]))
        return copies

    there = (stage, recv, a_send, a_recv, own_a)
    back = (stage2, recv2, b_send, b_recv, own_b)

    def send_blocks(c, _):
        for copy in block_copies(c, *there):
            copy.start()
        return 0

    lax.fori_loop(0, comps, send_blocks, 0)

    def flow_messages(slot):
        out = []
        for si, s in enumerate(SIGNS):
            for m, (oy, oz) in enumerate(X_OFFS):
                out.append(((s, oy, oz), XM.at[si], XH.at[slot, si, m]))
        for si, s in enumerate(SIGNS):
            out.append(((0, s, 0), YM.at[si], YH.at[slot, si]))
            for zi, z in enumerate(SIGNS):
                src = YM.at[si, 3 + zi, pl.ds(size_z - 8 if z > 0 else 0, 8)]
                out.append(((0, s, z), src, YE.at[slot, si, zi]))
        for si, s in enumerate(SIGNS):
            out.append(((0, 0, s), ZM.at[si], ZH.at[slot, si]))
        return out

    def solute_messages():
        out = []
        for ax in range(3):
            for si, s in enumerate(SIGNS):
                off = tuple(s if a == ax else 0 for a in range(3))
                out.append((off, SM.at[ax, si], SH.at[ax, si]))
        return out

    def exchange(messages, send, rec):
        copies = [
            pltpu.make_async_remote_copy(
                src_ref=src, dst_ref=dst, send_sem=send.at[k], recv_sem=rec(k),
                device_id=dev(off), device_id_type=pl.DeviceIdType.MESH)
            for k, (off, src, dst) in enumerate(messages)
        ]

        def start(which):
            for (off, _, _), copy in zip(messages, copies):
                if which(off):
                    @pl.when(exists(off))
                    def _(copy=copy):
                        copy.start()

        def finish():
            for (off, _, _), copy in zip(messages, copies):
                @pl.when(exists(tuple(-o for o in off)))
                def _(copy=copy):
                    copy.wait_recv()
            for (off, _, _), copy in zip(messages, copies):
                @pl.when(exists(off))
                def _(copy=copy):
                    copy.wait_send()
        return start, finish

    def z_face(off):
        return off[0] == 0 and off[1] == 0

    def not_z_face(off):
        return not z_face(off)

    def pack_x(z, planes, acc):
        new = []
        at_z = (lane & 15) == z
        for si, s in enumerate(SIGNS):
            w = None
            for j, v in enumerate(planes[si]):
                r = pltpu.roll(v, z + (16 * j + 1 if s > 0 else 16 * j), 1)
                w = r if w is None else jnp.where((lane >= 16 * j), r, w)
            new.append(jnp.where(at_z, w, acc[si]))
        return tuple(new)

    def pack_flow(z, values, acc):
        for si, s in enumerate(SIGNS):
            e = 15 if s > 0 else 0
            for j, d in enumerate(Y_SIDE[si]):
                YM[si, j, pl.ds(z, 1), :] = values[d][e:e + 1, :]
        return pack_x(z, [[values[d] for d in X_SIDE[si]] for si in range(2)], acc)

    def z_pack():
        for si, s in enumerate(SIGNS):
            for j, d in enumerate(Z_SIDE[si]):
                ZM[si, j] = F[d, size_z if s > 0 else 1]

    zero2 = (jnp.zeros((16, 128), jnp.float32),) * 2

    def flow_halo(slot):
        for si, s in enumerate(SIGNS):
            for j, d in enumerate(Z_SIDE[si]):
                F[d, 0 if s > 0 else size_z + 1] = ZH[slot, si, j]
            for zi, z in enumerate(SIGNS):
                base = YH[slot, si, 3 + zi]
                e = YE[slot, si, zi, 7:8, :] if z > 0 else YE[slot, si, zi, 0:1, :]
                edge = row == (15 if z > 0 else 0)
                YC[si, zi] = pltpu.roll(jnp.where(edge, jnp.broadcast_to(e, (16, 128)), base), 1 if z > 0 else 15, 0)
            base = XH[slot, si, 0]
            g1 = pltpu.roll(jnp.where(row == 15, XH[slot, si, 1], base), 1, 0)
            g2 = pltpu.roll(jnp.where(row == 0, XH[slot, si, 2], base), 15, 0)
            g3 = jnp.where(lane == 48, pltpu.roll(XH[slot, si, 3], 113, 1), pltpu.roll(base, 1, 1))
            g4 = jnp.where(lane == 79, pltpu.roll(XH[slot, si, 4], 15, 1), pltpu.roll(base, 127, 1))
            c = jnp.where(lane < 16, base, g1)
            c = jnp.where(lane < 32, c, g2)
            c = jnp.where(lane < 48, c, g3)
            XC[si] = jnp.where(lane < 64, c, g4)

    def shifted_flow(slot, z, xz):
        out = [None]
        for d in range(1, 19):
            cx, cy, cz = FLOW_DIRS[d]
            v = F[d, z + (1 - cz)]
            if cy:
                si = side(cy)
                j = Y_SIDE[si].index(d)
                if j < 3:
                    e = YH[slot, si, j, pl.ds(z, 1), :]
                else:
                    e = YC[si, j - 3, pl.ds(z, 1), :]
                v = jnp.where(row == (0 if cy > 0 else 15), jnp.broadcast_to(e, (16, 128)),
                              pltpu.roll(v, 1 if cy > 0 else 15, 0))
            if cx:
                si = side(cx)
                j = X_SIDE[si].index(d)
                if cx > 0:
                    h = pltpu.roll(xz[0], (128 - 16 * j) - z if j else lax.rem(128 - z, 128), 1)
                    v = jnp.where(lane == 0, h, pltpu.roll(v, 1, 1))
                else:
                    h = pltpu.roll(xz[1], (127 - 16 * j) - z, 1)
                    v = jnp.where(lane == 127, h, pltpu.roll(v, 127, 1))
            out.append(v)
        return out

    def moments(z, p, porous):
        density = p[0]
        for v in p[1:]:
            density = density + v
        inv = porous / density
        m = []
        for ax in range(3):
            total = None
            for d in range(1, 19):
                if FLOW_DIRS[d][ax] > 0:
                    diff = p[d] - p[OPP[d]]
                    total = diff if total is None else total + diff
            m.append(total * inv)
        U[0, z] = density
        for ax in range(3):
            U[1 + ax, z] = m[ax]

    loads[3].wait()
    loads[4].wait()

    def fill(z, acc):
        porous = mask_ref[z].astype(jnp.float32)
        for d in range(19):
            F[d, z + 1] = porous
        moments(z, [out_pop[d, z] for d in range(19)], porous)
        return pack_flow(z, [porous] * 19, acc)

    XM[0], XM[1] = planes_loop(size_z, fill, zero2)
    z_pack()
    start, finish = exchange(flow_messages(0), f_send, lambda k: f_recv.at[0, k])
    start(lambda off: True)
    finish()
    flow_halo(0)

    def link_bits(z, _):
        xz = [XC[0], XC[1]]
        moved = shifted_flow(0, z, xz)
        pore = mask_ref[z] > 0
        bits = jnp.where(pore, 1, 0)
        for d in range(1, 19):
            bits = bits | jnp.where(jnp.logical_and(pore, moved[d] > 0.5), 1 << d, 0)
        B[z] = bits
        return 0

    planes_loop(size_z, link_bits, 0)

    def place(c, _):
        for copy in block_copies(c, *there):
            copy.wait()
        for j in range(tiles):
            T[c, j * rows:(j + 1) * rows, :] = choose(tile_where[j], pairs_of(recv, c))
        for r in range(rows):
            v = T[c, pl.ds(r, tiles, stride=rows), :]
            G[c, r // 2, (r % 2) * 8:(r % 2) * 8 + 8, :] = swap_chunks(v)
        return 0

    lax.fori_loop(0, comps, place, 0)

    def unplace(c, _):
        for r in range(rows):
            T[c, pl.ds(r, tiles, stride=rows), :] = swap_chunks(G[c, r // 2, (r % 2) * 8:(r % 2) * 8 + 8, :])
        for q in range(n_z * cap):
            stage2[c, q // cap, q % cap] = choose(tile_pick[q], blocks_of(c, tiles))
        for copy in block_copies(c, *back):
            copy.start()
        return 0

    def collide_solute(z, acc):
        g = [G[i, z] for i in range(7)]
        u = [U[1 + a, z] for a in range(3)]
        conc = g[0]
        for v in g[1:]:
            conc = conc + v
        post = [g[0] * (1 - OMEGA_SOLUTE) + (OMEGA_SOLUTE * 0.25) * conc]
        cw = (OMEGA_SOLUTE * 0.125) * conc
        for i in range(1, 7):
            ax = (i - 1) // 2
            f = 1.0 + 4.0 * u[ax] if i % 2 else 1.0 - 4.0 * u[ax]
            post.append(g[i] * (1 - OMEGA_SOLUTE) + cw * f)
        for i in range(7):
            S[i, z + 1] = post[i]
        SM[1, 0, pl.ds(z, 1), :] = post[3][15:16, :]
        SM[1, 1, pl.ds(z, 1), :] = post[4][0:1, :]
        at_z = lane == z
        return (jnp.where(at_z, pltpu.roll(post[1], z + 1, 1), acc[0]),
                jnp.where(at_z, pltpu.roll(post[2], z, 1), acc[1]))

    def stream_solute(z, acc):
        bits = B[z]
        pore = (bits & 1) != 0
        xz = [SH[0, 0], SH[0, 1]]
        s = [S[i, z + 1] for i in range(7)]
        new = [s[0]]
        for i in range(1, 7):
            cx, cy, cz = FLOW_DIRS[i]
            if cx > 0:
                v = jnp.where(lane == 0, pltpu.roll(xz[0], lax.rem(128 - z, 128), 1), pltpu.roll(s[i], 1, 1))
            elif cx < 0:
                v = jnp.where(lane == 127, pltpu.roll(xz[1], 127 - z, 1), pltpu.roll(s[i], 127, 1))
            elif cy:
                e = SH[1, side(cy), pl.ds(z, 1), :]
                v = jnp.where(row == (0 if cy > 0 else 15), jnp.broadcast_to(e, (16, 128)),
                              pltpu.roll(s[i], 1 if cy > 0 else 15, 0))
            else:
                v = S[i, z + (1 - cz)]
            new.append(jnp.where((bits & (1 << i)) != 0, v, jnp.where(pore, s[OPP[i]], s[i])))
        for i in range(7):
            G[i, z] = new[i]
        return new

    def collide_flow(z, acc, new):
        pore = (B[z] & 1) != 0
        conc = new[0]
        for v in new[1:]:
            conc = conc + v
        rho = U[0, z]
        ux = U[1, z]
        uy = U[2, z]
        uz = U[3, z] + jnp.where(pore, FORCE_GAIN * (conc - REST_CONC), 0.0)
        base = 1.0 - 1.5 * (ux * ux + uy * uy + uz * uz)
        p = [out_pop[d, z] for d in range(19)]
        post = [None] * 19
        post[0] = jnp.where(pore, p[0] * (1 - OMEGA_FLOW) + (OMEGA_FLOW / 3.0) * rho * base, p[0])
        w1 = (OMEGA_FLOW / 18.0) * rho
        w2 = (OMEGA_FLOW / 36.0) * rho
        for d in range(1, 19, 2):
            o = OPP[d]
            along = None
            for c, u in zip(FLOW_DIRS[d], (ux, uy, uz)):
                if c:
                    along = (u if c > 0 else -u) if along is None else (along + u if c > 0 else along - u)
            w = w1 if d < 7 else w2
            even = base + 4.5 * along * along
            odd = 3.0 * along
            post[d] = jnp.where(pore, p[d] * (1 - OMEGA_FLOW) + w * (even + odd), p[d])
            post[o] = jnp.where(pore, p[o] * (1 - OMEGA_FLOW) + w * (even - odd), p[o])
        for d in range(19):
            F[d, z + 1] = post[d]
        return pack_flow(z, post, acc)

    def stream_flow(slot):
        def body(z, _):
            bits = B[z]
            pore = (bits & 1) != 0
            xz = [XC[0], XC[1]]
            moved = shifted_flow(slot, z, xz)
            here = [F[d, z + 1] for d in range(19)]
            p = [here[0]]
            for d in range(1, 19):
                p.append(jnp.where((bits & (1 << d)) != 0, moved[d], jnp.where(pore, here[OPP[d]], here[d])))
            for d in range(19):
                out_pop[d, z] = p[d]
            moments(z, p, jnp.where(pore, 1.0, 0.0))
            return 0
        planes_loop(size_z, body, 0)

    ends = (0, size_z - 1)

    def step(t, last):
        slot = lax.rem(t + 1, 2)
        start, finish = exchange(solute_messages(), s_send, lambda k: s_recv.at[k])
        acc = zero2
        for z in ends:
            acc = collide_solute(z, acc)
        for si in range(2):
            SM[2, si] = S[5 + si, size_z if si == 0 else 1]
        start(z_face)
        acc = planes_loop(size_z - 2, collide_solute, acc, 1, 7)
        SM[0, 0], SM[0, 1] = acc
        start(not_z_face)
        finish()
        S[5, 0] = SH[2, 0]
        S[6, size_z + 1] = SH[2, 1]
        if last:
            planes_loop(size_z, lambda z, _: (stream_solute(z, None), 0)[1], 0)
            lax.fori_loop(0, comps, unplace, 0)

        def collide(z, acc):
            new = [G[i, z] for i in range(7)] if last else stream_solute(z, None)
            return collide_flow(z, acc, new)

        start, finish = exchange(flow_messages(slot), f_send, lambda k: f_recv.at[slot, k])
        acc = zero2
        for z in ends:
            acc = collide(z, acc)
        z_pack()
        start(z_face)
        XM[0], XM[1] = planes_loop(size_z - 2, collide, acc, 1, 7)
        start(not_z_face)
        finish()
        flow_halo(slot)
        stream_flow(slot)

    lax.fori_loop(0, STEPS - 1, lambda t, _: (step(t, False), 0)[1], 0)
    step(jnp.int32(STEPS - 1), True)

    def deliver(c, _):
        for copy in block_copies(c, *back):
            copy.wait()
        for s in range(slots):
            T[c, s * rows:(s + 1) * rows, :] = choose(slot_where[s], pairs_of(recv2, c))
        for r in range(rows):
            out_sol[c, :, r * 128:(r + 1) * 128] = T[c, pl.ds(r, slots, stride=rows), :]
        return 0

    lax.fori_loop(0, comps, deliver, 0)


def shards(sizes, populations, solute_state, pore_mask, block_slot, slot_block):
    n_z = sizes[2]
    tiles = block_slot.shape[2]
    cap = -(-tiles // n_z)
    comps, slots, cells = solute_state.shape
    rows = cells // 128
    sz, sy, sx = pore_mask.shape
    f32 = jnp.float32
    blocks = pltpu.VMEM((comps, n_z, cap, rows, 128), f32)
    dma = pltpu.SemaphoreType.DMA
    hbm = pl.BlockSpec(memory_space=pltpu.HBM)
    vmem = pl.BlockSpec(memory_space=pltpu.VMEM)
    return pl.pallas_call(
        functools.partial(kernel, sizes, cap),
        out_shape=(
            jax.ShapeDtypeStruct(populations.shape, f32),
            jax.ShapeDtypeStruct(solute_state.shape, f32),
        ),
        in_specs=[hbm] * 5,
        out_specs=(vmem, vmem),
        scratch_shapes=[
            pltpu.VMEM(solute_state.shape, f32),
            pltpu.VMEM(pore_mask.shape, jnp.int32),
            pltpu.SMEM(block_slot.shape, jnp.int32),
            pltpu.SMEM(slot_block.shape, jnp.int32),
            pltpu.VMEM((19, sz + 2, sy, sx), f32),
            pltpu.VMEM((7, sz, sy, sx), f32),
            pltpu.VMEM((7, sz + 2, sy, sx), f32),
            pltpu.VMEM((4, sz, sy, sx), f32),
            pltpu.VMEM((sz, sy, sx), jnp.int32),
            pltpu.VMEM((2, 16, 128), f32),
            pltpu.VMEM((2, 5, 16, 128), f32),
            pltpu.VMEM((2, 5, 16, 128), f32),
            pltpu.VMEM((2, 2, 5, 16, 128), f32),
            pltpu.VMEM((2, 2, 5, 16, 128), f32),
            pltpu.VMEM((2, 2, 2, 8, 128), f32),
            pltpu.VMEM((2, 2, 5, 16, 128), f32),
            pltpu.VMEM((2, 16, 128), f32),
            pltpu.VMEM((2, 2, 16, 128), f32),
            pltpu.VMEM((3, 2, 16, 128), f32),
            pltpu.VMEM((3, 2, 16, 128), f32),
            pltpu.VMEM((comps, slots * rows, 128), f32),
            blocks, blocks, blocks, blocks,
            dma((18,)), dma((2, 18)), dma((6,)), dma((6,)),
            dma((n_z, comps)), dma((n_z, comps)), dma((n_z, comps)), dma((n_z, comps)),
            dma((comps,)), dma((comps,)), dma((5,)),
        ],
        compiler_params=pltpu.CompilerParams(
            collective_id=0, has_side_effects=True, vmem_limit_bytes=32 * 1024 * 1024),
    )(populations, solute_state, pore_mask, block_slot, slot_block)


def solution(mesh):
    sizes = tuple(mesh.shape[a] for a in AXES)
    in_specs = (
        P(None, "gz", "gy", "gx"),
        P(None, ("gx", "gy", "gz"), None),
        P("gz", "gy", "gx"),
        P("gz", "gy", "gx"),
        P(("gx", "gy", "gz")),
    )
    out_specs = (P(None, "gz", "gy", "gx"), P(None, ("gx", "gy", "gz"), None))
    return jax.shard_map(
        functools.partial(shards, sizes), mesh=mesh, in_specs=in_specs, out_specs=out_specs, check_vma=False)
```

```python
import functools

import jax
import jax.numpy as jnp
from jax import lax
from jax.experimental import pallas as pl
from jax.experimental.pallas import tpu as pltpu
from jax.sharding import PartitionSpec as P

STEPS = 4
AXES = ("gx", "gy", "gz")

FLOW_DIRS = [
    (0, 0, 0),
    (1, 0, 0),
    (-1, 0, 0),
    (0, 1, 0),
    (0, -1, 0),
    (0, 0, 1),
    (0, 0, -1),
    (1, 1, 0),
    (-1, -1, 0),
    (1, -1, 0),
    (-1, 1, 0),
    (1, 0, 1),
    (-1, 0, -1),
    (1, 0, -1),
    (-1, 0, 1),
    (0, 1, 1),
    (0, -1, -1),
    (0, 1, -1),
    (0, -1, 1),
]
FLOW_WEIGHTS = [1.0 / 3.0] + [1.0 / 18.0] * 6 + [1.0 / 36.0] * 12
OPP = [FLOW_DIRS.index((-a, -b, -c)) for a, b, c in FLOW_DIRS]
OMEGA_FLOW = 1.2
OMEGA_SOLUTE = 1.5
FORCE_GAIN = 0.02
REST_CONC = 8.0
SIGNS = (1, -1)

X_SIDE = [[FLOW_DIRS.index((s, b, c)) for b, c in ((0, 0), (1, 0), (-1, 0), (0, 1), (0, -1))] for s in SIGNS]
Y_SIDE = [[FLOW_DIRS.index((a, s, c)) for a, c in ((0, 0), (1, 0), (-1, 0), (0, 1), (0, -1))] for s in SIGNS]
Z_SIDE = [[FLOW_DIRS.index((a, b, s)) for a, b in ((0, 0), (1, 0), (-1, 0), (0, 1), (0, -1))] for s in SIGNS]
X_OFFS = [(0, 0), (1, 0), (-1, 0), (0, 1), (0, -1)]


def side(sign):
    return 0 if sign > 0 else 1


def planes_loop(n, body, init, first=0, unroll=4):
    def group(g, acc):
        for k in range(unroll):
            acc = body(first + g * unroll + k, acc)
        return acc
    return lax.fori_loop(0, n // unroll, group, init)


def iota(axis, shape=(16, 128)):
    return lax.broadcasted_iota(jnp.int32, shape, axis)


def swap_chunks(v):
    sub = iota(0, (8, 128))
    chunk = lax.shift_right_logical(iota(1, (8, 128)), 4)
    for k in (1, 2, 4):
        sbit = (sub & k) != 0
        if k == 4:
            both = pltpu.roll(pltpu.roll(v, 64, 1), 4, 0)
            v = jnp.where(((sub ^ chunk) & k) == 0, v, both)
        else:
            up = pltpu.roll(pltpu.roll(v, 16 * k, 1), 8 - k, 0)
            down = pltpu.roll(pltpu.roll(v, 128 - 16 * k, 1), k, 0)
            same = ((sub ^ chunk) & k) == 0
            v = jnp.where(same, v, jnp.where(sbit, down, up))
    return v


def kernel(
    sizes, cap, pop_hbm, sol_hbm, mask_hbm, bs_hbm, sb_hbm, pop_out, sol_out,
    out_pop, out_sol, sol_ref, mask_ref, bs_ref, sb_ref,
    F, G, S, U, B, XM, YM, ZM, XH, YH, YE, ZH, XC, YC, SM, SH,
    T, stage, recv, stage2, recv2,
    f_send, f_recv, s_send, s_recv, a_send, a_recv, b_send, b_recv, own_a, own_b, io_sem, sol_sem,
):
    n_x, n_y, n_z = sizes
    loads = [
        pltpu.make_async_copy(src, dst, io_sem.at[k])
        for k, (src, dst) in enumerate((
            (sb_hbm, sb_ref), (bs_hbm, bs_ref), (sol_hbm, sol_ref), (mask_hbm, mask_ref), (pop_hbm, out_pop)))
    ]
    for load in loads:
        load.start()
    me = tuple(lax.axis_index(a) for a in AXES)
    lane = iota(1)
    row = iota(0)
    size_z = mask_ref.shape[0] // 16
    slots = sb_ref.shape[0]
    tiles = bs_ref.shape[2]
    comps = sol_ref.shape[0]

    def rows_of(z):
        return pl.ds(z * 16 if isinstance(z, int) else pl.multiple_of(z * 16, 16), 16)

    def exists(off):
        ok = None
        for pos, n, o in zip(me, sizes, off):
            if o == 0:
                continue
            c = (pos + o < n) if o > 0 else (pos >= 1)
            ok = c if ok is None else jnp.logical_and(ok, c)
        return ok

    def dev(off):
        return {a: p + o for a, p, o in zip(AXES, me, off)}

    neighbours = [c for c in FLOW_DIRS[1:]]

    XH[0] = jnp.zeros_like(XH[0])
    YH[0] = jnp.zeros_like(YH[0])
    YE[0] = jnp.zeros_like(YE[0])
    ZH[0] = jnp.zeros_like(ZH[0])

    barrier = pltpu.get_barrier_semaphore()
    count = jnp.int32(n_z - 1)
    for off in neighbours:
        if off[0] == 0 and off[1] == 0:
            continue
        ok = exists(off)
        count = count + ok.astype(jnp.int32)

        @pl.when(ok)
        def _(off=off):
            pl.semaphore_signal(barrier, inc=1, device_id=dev(off), device_id_type=pl.DeviceIdType.MESH)

    for k in range(1, n_z):
        other = lax.rem(me[2] + k, n_z)
        pl.semaphore_signal(
            barrier, inc=1, device_id={"gx": me[0], "gy": me[1], "gz": other},
            device_id_type=pl.DeviceIdType.MESH)

    def routing(values, per):
        group = [lax.div(jnp.maximum(v, 0), jnp.int32(per)) for v in values]
        held = [(v >= 0).astype(jnp.int32) for v in values]
        rank = []
        for s in range(len(values)):
            r = jnp.int32(0)
            for e in range(s):
                r = r + jnp.where(group[e] == group[s], held[e], 0)
            rank.append(r)
        pick = []
        for g in range(n_z):
            for p in range(cap):
                at = jnp.int32(0)
                for s in range(len(values)):
                    hit = jnp.logical_and(group[s] == g, rank[s] == p)
                    at = at + jnp.where(hit, held[s] * s, 0)
                pick.append(at)
        where = [(group[s] * cap + rank[s] + 1) * held[s] - 1 for s in range(len(values))]
        return pick, where

    loads[0].wait()
    loads[1].wait()
    slot_pick, slot_where = routing([sb_ref[s] for s in range(slots)], tiles)
    tile_pick, tile_where = routing([bs_ref[0, 0, j] for j in range(tiles)], slots)
    rows = T.shape[1] // slots

    def blocks_of(c, n):
        return [T[c, k * rows:(k + 1) * rows, :] for k in range(n)]

    def pairs_of(buf, c):
        return [buf[c, q // cap, q % cap] for q in range(n_z * cap)]

    def choose(index, options):
        at = jnp.full(options[0].shape, index, jnp.int32)
        out = jnp.zeros_like(options[0])
        for k, v in enumerate(options):
            out = jnp.where(at == k, v, out)
        return out

    def gather(c, _):
        for r in range(rows):
            T[c, pl.ds(r, slots, stride=rows), :] = sol_ref[c, :, r * 128:(r + 1) * 128]
        for q in range(n_z * cap):
            stage[c, q // cap, q % cap] = choose(slot_pick[q], blocks_of(c, slots))
        return 0

    loads[2].wait()
    lax.fori_loop(0, comps, gather, 0)
    pl.semaphore_wait(barrier, count)

    hops = sorted(range(1, n_z), key=lambda k: abs(2 * k - n_z))

    def block_copies(c, src, dst, send, rec, own):
        copies = []
        for k in hops:
            other = lax.rem(me[2] + k, n_z)
            copies.append(pltpu.make_async_remote_copy(
                src_ref=src.at[c, other], dst_ref=dst.at[c, me[2]],
                send_sem=send.at[k, c], recv_sem=rec.at[k, c],
                device_id={"gx": me[0], "gy": me[1], "gz": other},
                device_id_type=pl.DeviceIdType.MESH))
        copies.append(pltpu.make_async_copy(src.at[c, me[2]], dst.at[c, me[2]], own.at[c]))
        return copies

    there = (stage, recv, a_send, a_recv, own_a)
    back = (stage2, recv2, b_send, b_recv, own_b)

    def send_blocks(c, _):
        for copy in block_copies(c, *there):
            copy.start()
        return 0

    lax.fori_loop(0, comps, send_blocks, 0)

    def flow_messages(slot):
        out = []
        for si, s in enumerate(SIGNS):
            for m, (oy, oz) in enumerate(X_OFFS):
                out.append(((s, oy, oz), XM.at[si], XH.at[slot, si, m]))
        for si, s in enumerate(SIGNS):
            out.append(((0, s, 0), YM.at[si], YH.at[slot, si]))
            for zi, z in enumerate(SIGNS):
                src = YM.at[si, 3 + zi, pl.ds(size_z - 8 if z > 0 else 0, 8)]
                out.append(((0, s, z), src, YE.at[slot, si, zi]))
        for si, s in enumerate(SIGNS):
            out.append(((0, 0, s), ZM.at[si], ZH.at[slot, si]))
        return out

    def solute_messages():
        out = []
        for ax in range(3):
            for si, s in enumerate(SIGNS):
                off = tuple(s if a == ax else 0 for a in range(3))
                out.append((off, SM.at[ax, si], SH.at[ax, si]))
        return out

    def exchange(messages, send, rec):
        copies = [
            pltpu.make_async_remote_copy(
                src_ref=src, dst_ref=dst, send_sem=send.at[k], recv_sem=rec(k),
                device_id=dev(off), device_id_type=pl.DeviceIdType.MESH)
            for k, (off, src, dst) in enumerate(messages)
        ]

        def start(which):
            for (off, _, _), copy in zip(messages, copies):
                if which(off):
                    @pl.when(exists(off))
                    def _(copy=copy):
                        copy.start()

        def finish():
            for (off, _, _), copy in zip(messages, copies):
                @pl.when(exists(tuple(-o for o in off)))
                def _(copy=copy):
                    copy.wait_recv()
            for (off, _, _), copy in zip(messages, copies):
                @pl.when(exists(off))
                def _(copy=copy):
                    copy.wait_send()
        return start, finish

    def z_face(off):
        return off[0] == 0 and off[1] == 0

    def not_z_face(off):
        return not z_face(off)

    def pack_x(z, planes, acc):
        new = []
        at_z = (lane & 15) == z
        for si, s in enumerate(SIGNS):
            w = None
            for j, v in enumerate(planes[si]):
                r = pltpu.roll(v, z + (16 * j + 1 if s > 0 else 16 * j), 1)
                w = r if w is None else jnp.where((lane >= 16 * j), r, w)
            new.append(jnp.where(at_z, w, acc[si]))
        return tuple(new)

    def pack_flow(z, values, acc):
        for si, s in enumerate(SIGNS):
            e = 15 if s > 0 else 0
            for j, d in enumerate(Y_SIDE[si]):
                YM[si, j, pl.ds(z, 1), :] = values[d][e:e + 1, :]
        return pack_x(z, [[values[d] for d in X_SIDE[si]] for si in range(2)], acc)

    def z_pack():
        for si, s in enumerate(SIGNS):
            for j, d in enumerate(Z_SIDE[si]):
                ZM[si, j] = F[d, size_z if s > 0 else 1]

    zero2 = (jnp.zeros((16, 128), jnp.float32),) * 2

    def z_halo(slot):
        for si, s in enumerate(SIGNS):
            for j, d in enumerate(Z_SIDE[si]):
                F[d, 0 if s > 0 else size_z + 1] = ZH[slot, si, j]

    def flow_halo(slot):
        for si, s in enumerate(SIGNS):
            for zi, z in enumerate(SIGNS):
                base = YH[slot, si, 3 + zi]
                e = YE[slot, si, zi, 7:8, :] if z > 0 else YE[slot, si, zi, 0:1, :]
                edge = row == (15 if z > 0 else 0)
                YC[si, zi] = pltpu.roll(jnp.where(edge, jnp.broadcast_to(e, (16, 128)), base), 1 if z > 0 else 15, 0)
            base = XH[slot, si, 0]
            g1 = pltpu.roll(jnp.where(row == 15, XH[slot, si, 1], base), 1, 0)
            g2 = pltpu.roll(jnp.where(row == 0, XH[slot, si, 2], base), 15, 0)
            g3 = jnp.where(lane == 48, pltpu.roll(XH[slot, si, 3], 113, 1), pltpu.roll(base, 1, 1))
            g4 = jnp.where(lane == 79, pltpu.roll(XH[slot, si, 4], 15, 1), pltpu.roll(base, 127, 1))
            c = jnp.where(lane < 16, base, g1)
            c = jnp.where(lane < 32, c, g2)
            c = jnp.where(lane < 48, c, g3)
            XC[si] = jnp.where(lane < 64, c, g4)

    def shifted_flow(slot, z, xz):
        out = [None]
        for d in range(1, 19):
            cx, cy, cz = FLOW_DIRS[d]
            v = F[d, z + (1 - cz)]
            if cy:
                si = side(cy)
                j = Y_SIDE[si].index(d)
                if j < 3:
                    e = YH[slot, si, j, pl.ds(z, 1), :]
                else:
                    e = YC[si, j - 3, pl.ds(z, 1), :]
                v = jnp.where(row == (0 if cy > 0 else 15), jnp.broadcast_to(e, (16, 128)),
                              pltpu.roll(v, 1 if cy > 0 else 15, 0))
            if cx:
                si = side(cx)
                j = X_SIDE[si].index(d)
                if cx > 0:
                    h = pltpu.roll(xz[0], (128 - 16 * j) - z if j else lax.rem(128 - z, 128), 1)
                    v = jnp.where(lane == 0, h, pltpu.roll(v, 1, 1))
                else:
                    h = pltpu.roll(xz[1], (127 - 16 * j) - z, 1)
                    v = jnp.where(lane == 127, h, pltpu.roll(v, 127, 1))
            out.append(v)
        return out

    def moments(z, p, porous):
        density = p[0]
        for v in p[1:]:
            density = density + v
        inv = porous / density
        m = []
        for ax in range(3):
            total = None
            for d in range(1, 19):
                if FLOW_DIRS[d][ax] > 0:
                    diff = p[d] - p[OPP[d]]
                    total = diff if total is None else total + diff
            m.append(total * inv)
        U[0, z] = density
        for ax in range(3):
            U[1 + ax, z] = m[ax]

    loads[3].wait()
    loads[4].wait()

    def fill(z, acc):
        porous = mask_ref[rows_of(z), :].astype(jnp.float32)
        for d in range(19):
            F[d, z + 1] = porous
        moments(z, [out_pop[d, rows_of(z), :] for d in range(19)], porous)
        return pack_flow(z, [porous] * 19, acc)

    XM[0], XM[1] = planes_loop(size_z, fill, zero2)
    z_pack()
    start, finish = exchange(flow_messages(0), f_send, lambda k: f_recv.at[0, k])
    start(lambda off: True)
    finish()
    z_halo(0)
    flow_halo(0)

    def link_bits(z, _):
        xz = [XC[0], XC[1]]
        moved = shifted_flow(0, z, xz)
        pore = mask_ref[rows_of(z), :] > 0
        bits = jnp.where(pore, 1, 0)
        for d in range(1, 19):
            bits = bits | jnp.where(jnp.logical_and(pore, moved[d] > 0.5), 1 << d, 0)
        B[rows_of(z), :] = bits
        return 0

    planes_loop(size_z, link_bits, 0)

    def place(c, _):
        for copy in block_copies(c, *there):
            copy.wait()
        for j in range(tiles):
            T[c, j * rows:(j + 1) * rows, :] = choose(tile_where[j], pairs_of(recv, c))
        for r in range(rows):
            v = T[c, pl.ds(r, tiles, stride=rows), :]
            G[c, r // 2, (r % 2) * 8:(r % 2) * 8 + 8, :] = swap_chunks(v)
        return 0

    lax.fori_loop(0, comps, place, 0)

    def unplace(c, _):
        for r in range(rows):
            T[c, pl.ds(r, tiles, stride=rows), :] = swap_chunks(G[c, r // 2, (r % 2) * 8:(r % 2) * 8 + 8, :])
        for q in range(n_z * cap):
            stage2[c, q // cap, q % cap] = choose(tile_pick[q], blocks_of(c, tiles))
        for copy in block_copies(c, *back):
            copy.start()
        return 0

    def collide_solute(z, acc):
        g = [G[i, z] for i in range(7)]
        u = [U[1 + a, z] for a in range(3)]
        conc = g[0]
        for v in g[1:]:
            conc = conc + v
        post = [g[0] * (1 - OMEGA_SOLUTE) + (OMEGA_SOLUTE * 0.25) * conc]
        cw = (OMEGA_SOLUTE * 0.125) * conc
        for i in range(1, 7):
            ax = (i - 1) // 2
            f = 1.0 + 4.0 * u[ax] if i % 2 else 1.0 - 4.0 * u[ax]
            post.append(g[i] * (1 - OMEGA_SOLUTE) + cw * f)
        for i in range(7):
            S[i, z + 1] = post[i]
        SM[1, 0, pl.ds(z, 1), :] = post[3][15:16, :]
        SM[1, 1, pl.ds(z, 1), :] = post[4][0:1, :]
        at_z = lane == z
        return (jnp.where(at_z, pltpu.roll(post[1], z + 1, 1), acc[0]),
                jnp.where(at_z, pltpu.roll(post[2], z, 1), acc[1]))

    def stream_solute(z, acc):
        bits = B[rows_of(z), :]
        pore = (bits & 1) != 0
        xz = [SH[0, 0], SH[0, 1]]
        s = [S[i, z + 1] for i in range(7)]
        new = [s[0]]
        for i in range(1, 7):
            cx, cy, cz = FLOW_DIRS[i]
            if cx > 0:
                v = jnp.where(lane == 0, pltpu.roll(xz[0], lax.rem(128 - z, 128), 1), pltpu.roll(s[i], 1, 1))
            elif cx < 0:
                v = jnp.where(lane == 127, pltpu.roll(xz[1], 127 - z, 1), pltpu.roll(s[i], 127, 1))
            elif cy:
                e = SH[1, side(cy), pl.ds(z, 1), :]
                v = jnp.where(row == (0 if cy > 0 else 15), jnp.broadcast_to(e, (16, 128)),
                              pltpu.roll(s[i], 1 if cy > 0 else 15, 0))
            else:
                v = S[i, z + (1 - cz)]
            new.append(jnp.where((bits & (1 << i)) != 0, v, jnp.where(pore, s[OPP[i]], s[i])))
        for i in range(7):
            G[i, z] = new[i]
        return new

    def collide_flow(z, acc, new):
        pore = (B[rows_of(z), :] & 1) != 0
        conc = new[0]
        for v in new[1:]:
            conc = conc + v
        rho = U[0, z]
        ux = U[1, z]
        uy = U[2, z]
        uz = U[3, z] + jnp.where(pore, FORCE_GAIN * (conc - REST_CONC), 0.0)
        base = 1.0 - 1.5 * (ux * ux + uy * uy + uz * uz)
        p = [out_pop[d, rows_of(z), :] for d in range(19)]
        post = [None] * 19
        post[0] = jnp.where(pore, p[0] * (1 - OMEGA_FLOW) + (OMEGA_FLOW / 3.0) * rho * base, p[0])
        w1 = (OMEGA_FLOW / 18.0) * rho
        w2 = (OMEGA_FLOW / 36.0) * rho
        for d in range(1, 19, 2):
            o = OPP[d]
            along = None
            for c, u in zip(FLOW_DIRS[d], (ux, uy, uz)):
                if c:
                    along = (u if c > 0 else -u) if along is None else (along + u if c > 0 else along - u)
            w = w1 if d < 7 else w2
            even = base + 4.5 * along * along
            odd = 3.0 * along
            post[d] = jnp.where(pore, p[d] * (1 - OMEGA_FLOW) + w * (even + odd), p[d])
            post[o] = jnp.where(pore, p[o] * (1 - OMEGA_FLOW) + w * (even - odd), p[o])
        for d in range(19):
            F[d, z + 1] = post[d]
        return pack_flow(z, post, acc)

    def shift_in_plane(d, v):
        cx, cy, _ = FLOW_DIRS[d]
        if cy:
            v = pltpu.roll(v, 1 if cy > 0 else 15, 0)
        if cx:
            v = pltpu.roll(v, 1 if cx > 0 else 127, 1)
        return v

    def stream_inside(z, _):
        bits = B[rows_of(z), :]
        pore = (bits & 1) != 0
        here = [F[d, z + 1] for d in range(19)]
        out_pop[0, rows_of(z), :] = here[0]
        for d in range(1, 19):
            cz = FLOW_DIRS[d][2]
            v = shift_in_plane(d, F[d, z + (1 - cz)] if cz else here[d])
            out_pop[d, rows_of(z), :] = jnp.where(
                (bits & (1 << d)) != 0, v, jnp.where(pore, here[OPP[d]], here[d]))
        return 0

    def edges_yz(slot):
        for si, s in enumerate(SIGNS):
            z = 0 if s > 0 else size_z - 1
            bits = B[rows_of(z), :]
            for j, d in enumerate(Z_SIDE[si]):
                v = shift_in_plane(d, ZH[slot, si, j])
                out_pop[d, rows_of(z), :] = jnp.where((bits & (1 << d)) != 0, v, out_pop[d, rows_of(z), :])
        for si, s in enumerate(SIGNS):
            at = pl.ds(0 if s > 0 else 15, size_z, stride=16)
            bits = B[at, :]
            for j, d in enumerate(Y_SIDE[si]):
                cx = FLOW_DIRS[d][0]
                v = YH[slot, si, j] if j < 3 else YC[si, j - 3]
                if cx:
                    v = pltpu.roll(v, 1 if cx > 0 else 127, 1)
                out_pop[d, at, :] = jnp.where((bits & (1 << d)) != 0, v, out_pop[d, at, :])

    def edge_x(z):
        bits = B[rows_of(z), :]
        p = [out_pop[d, rows_of(z), :] for d in range(19)]
        for si, s in enumerate(SIGNS):
            edge = jnp.where(lane == (0 if s > 0 else 127), bits, 0)
            for j, d in enumerate(X_SIDE[si]):
                back = (128 if s > 0 else 127) - 16 * j - z
                if s > 0 and j == 0:
                    back = lax.rem(back, 128)
                p[d] = jnp.where((edge & (1 << d)) != 0, pltpu.roll(XC[si], back, 1), p[d])
                out_pop[d, rows_of(z), :] = p[d]
        return p, bits

    def edge_x_collide(z, acc):
        p, bits = edge_x(z)
        moments(z, p, jnp.where((bits & 1) != 0, 1.0, 0.0))
        return collide_solute(z, acc)

    def solute_post(body):
        SM[0, 0], SM[0, 1] = planes_loop(size_z, body, zero2)
        for si in range(2):
            SM[2, si] = S[5 + si, size_z if si == 0 else 1]

    def step(t, last):
        slot = lax.rem(t + 1, 2)
        start, finish = exchange(solute_messages(), s_send, lambda k: s_recv.at[k])
        start(lambda off: True)
        finish()
        S[5, 0] = SH[2, 0]
        S[6, size_z + 1] = SH[2, 1]
        if last:
            planes_loop(size_z, lambda z, _: (stream_solute(z, None), 0)[1], 0)
            lax.fori_loop(0, comps, unplace, 0)

        def collide(z, acc):
            new = [G[i, z] for i in range(7)] if last else stream_solute(z, None)
            return collide_flow(z, acc, new)

        XM[0], XM[1] = planes_loop(size_z, collide, zero2)
        z_pack()
        start, finish = exchange(flow_messages(slot), f_send, lambda k: f_recv.at[slot, k])
        start(z_face)
        start(not_z_face)
        planes_loop(size_z, stream_inside, 0)
        finish()
        flow_halo(slot)
        edges_yz(slot)
        if last:
            planes_loop(size_z, lambda z, _: (edge_x(z), 0)[1], 0)
        else:
            solute_post(edge_x_collide)

    solute_post(collide_solute)
    lax.fori_loop(0, STEPS - 1, lambda t, _: (step(t, False), 0)[1], 0)
    step(jnp.int32(STEPS - 1), True)
    store_pop = pltpu.make_async_copy(out_pop, pop_out, io_sem.at[5])
    store_pop.start()

    def deliver(c, _):
        for copy in block_copies(c, *back):
            copy.wait()
        for s in range(slots):
            T[c, s * rows:(s + 1) * rows, :] = choose(slot_where[s], pairs_of(recv2, c))
        for r in range(rows):
            out_sol[c, :, r * 128:(r + 1) * 128] = T[c, pl.ds(r, slots, stride=rows), :]
        pltpu.make_async_copy(out_sol.at[c], sol_out.at[c], sol_sem.at[c]).start()
        return 0

    lax.fori_loop(0, comps, deliver, 0)
    for c in range(comps):
        pltpu.make_async_copy(out_sol.at[c], sol_out.at[c], sol_sem.at[c]).wait()
    store_pop.wait()


def shards(sizes, populations, solute_state, pore_mask, block_slot, slot_block):
    n_z = sizes[2]
    tiles = block_slot.shape[2]
    cap = -(-tiles // n_z)
    comps, slots, cells = solute_state.shape
    rows = cells // 128
    sz, sy, sx = pore_mask.shape
    f32 = jnp.float32
    blocks = pltpu.VMEM((comps, n_z, cap, rows, 128), f32)
    dma = pltpu.SemaphoreType.DMA
    hbm = pl.BlockSpec(memory_space=pl.ANY)
    new_populations, new_solute = pl.pallas_call(
        functools.partial(kernel, sizes, cap),
        out_shape=(
            jax.ShapeDtypeStruct((19, sz * sy, sx), f32),
            jax.ShapeDtypeStruct(solute_state.shape, f32),
        ),
        in_specs=[hbm] * 5,
        out_specs=(hbm, hbm),
        scratch_shapes=[
            pltpu.VMEM((19, sz * sy, sx), f32),
            pltpu.VMEM(solute_state.shape, f32),
            pltpu.VMEM(solute_state.shape, f32),
            pltpu.VMEM((sz * sy, sx), jnp.int32),
            pltpu.SMEM(block_slot.shape, jnp.int32),
            pltpu.SMEM(slot_block.shape, jnp.int32),
            pltpu.VMEM((19, sz + 2, sy, sx), f32),
            pltpu.VMEM((7, sz, sy, sx), f32),
            pltpu.VMEM((7, sz + 2, sy, sx), f32),
            pltpu.VMEM((4, sz, sy, sx), f32),
            pltpu.VMEM((sz * sy, sx), jnp.int32),
            pltpu.VMEM((2, 16, 128), f32),
            pltpu.VMEM((2, 5, 16, 128), f32),
            pltpu.VMEM((2, 5, 16, 128), f32),
            pltpu.VMEM((2, 2, 5, 16, 128), f32),
            pltpu.VMEM((2, 2, 5, 16, 128), f32),
            pltpu.VMEM((2, 2, 2, 8, 128), f32),
            pltpu.VMEM((2, 2, 5, 16, 128), f32),
            pltpu.VMEM((2, 16, 128), f32),
            pltpu.VMEM((2, 2, 16, 128), f32),
            pltpu.VMEM((3, 2, 16, 128), f32),
            pltpu.VMEM((3, 2, 16, 128), f32),
            pltpu.VMEM((comps, slots * rows, 128), f32),
            blocks, blocks, blocks, blocks,
            dma((18,)), dma((2, 18)), dma((6,)), dma((6,)),
            dma((n_z, comps)), dma((n_z, comps)), dma((n_z, comps)), dma((n_z, comps)),
            dma((comps,)), dma((comps,)), dma((6,)), dma((comps,)),
        ],
        compiler_params=pltpu.CompilerParams(
            collective_id=0, has_side_effects=True, vmem_limit_bytes=56 * 1024 * 1024),
    )(populations.reshape(19, sz * sy, sx), solute_state, pore_mask.reshape(sz * sy, sx), block_slot, slot_block)
    return new_populations.reshape(populations.shape), new_solute


def solution(mesh):
    sizes = tuple(mesh.shape[a] for a in AXES)
    in_specs = (
        P(None, "gz", "gy", "gx"),
        P(None, ("gx", "gy", "gz"), None),
        P("gz", "gy", "gx"),
        P("gz", "gy", "gx"),
        P(("gx", "gy", "gz")),
    )
    out_specs = (P(None, "gz", "gy", "gx"), P(None, ("gx", "gy", "gz"), None))
    return jax.shard_map(
        functools.partial(shards, sizes), mesh=mesh, in_specs=in_specs, out_specs=out_specs, check_vma=False)
```

```python
import functools

import jax
import jax.numpy as jnp
from jax import lax
from jax.experimental import pallas as pl
from jax.experimental.pallas import tpu as pltpu
from jax.sharding import PartitionSpec as P

STEPS = 4
AXES = ("gx", "gy", "gz")

FLOW_DIRS = [
    (0, 0, 0),
    (1, 0, 0),
    (-1, 0, 0),
    (0, 1, 0),
    (0, -1, 0),
    (0, 0, 1),
    (0, 0, -1),
    (1, 1, 0),
    (-1, -1, 0),
    (1, -1, 0),
    (-1, 1, 0),
    (1, 0, 1),
    (-1, 0, -1),
    (1, 0, -1),
    (-1, 0, 1),
    (0, 1, 1),
    (0, -1, -1),
    (0, 1, -1),
    (0, -1, 1),
]
FLOW_WEIGHTS = [1.0 / 3.0] + [1.0 / 18.0] * 6 + [1.0 / 36.0] * 12
OPP = [FLOW_DIRS.index((-a, -b, -c)) for a, b, c in FLOW_DIRS]
OMEGA_FLOW = 1.2
OMEGA_SOLUTE = 1.5
FORCE_GAIN = 0.02
REST_CONC = 8.0
SIGNS = (1, -1)

X_SIDE = [[FLOW_DIRS.index((s, b, c)) for b, c in ((0, 0), (1, 0), (-1, 0), (0, 1), (0, -1))] for s in SIGNS]
Y_SIDE = [[FLOW_DIRS.index((a, s, c)) for a, c in ((0, 0), (1, 0), (-1, 0), (0, 1), (0, -1))] for s in SIGNS]
Z_SIDE = [[FLOW_DIRS.index((a, b, s)) for a, b in ((0, 0), (1, 0), (-1, 0), (0, 1), (0, -1))] for s in SIGNS]
X_OFFS = [(0, 0), (1, 0), (-1, 0), (0, 1), (0, -1)]


def side(sign):
    return 0 if sign > 0 else 1


def planes_loop(n, body, init, first=0, unroll=4):
    def group(g, acc):
        for k in range(unroll):
            acc = body(first + g * unroll + k, acc)
        return acc
    return lax.fori_loop(0, n // unroll, group, init)


def iota(axis, shape=(16, 128)):
    return lax.broadcasted_iota(jnp.int32, shape, axis)


def swap_chunks(v):
    sub = iota(0, (8, 128))
    chunk = lax.shift_right_logical(iota(1, (8, 128)), 4)
    for k in (1, 2, 4):
        sbit = (sub & k) != 0
        if k == 4:
            both = pltpu.roll(pltpu.roll(v, 64, 1), 4, 0)
            v = jnp.where(((sub ^ chunk) & k) == 0, v, both)
        else:
            up = pltpu.roll(pltpu.roll(v, 16 * k, 1), 8 - k, 0)
            down = pltpu.roll(pltpu.roll(v, 128 - 16 * k, 1), k, 0)
            same = ((sub ^ chunk) & k) == 0
            v = jnp.where(same, v, jnp.where(sbit, down, up))
    return v


def kernel(
    sizes, cap, pop_hbm, sol_hbm, mask_hbm, bs_hbm, sb_hbm, pop_out, sol_out,
    out_pop, out_sol, sol_ref, mask_ref, bs_ref, sb_ref,
    F, G, S, U, B, XM, YM, ZM, XH, YH, YE, ZH, XC, YC, SM, SH,
    T, stage, recv, stage2, recv2,
    f_send, f_recv, s_send, s_recv, a_send, a_recv, b_send, b_recv, own_sem, io_sem, sol_sem,
):
    n_x, n_y, n_z = sizes
    loads = [
        pltpu.make_async_copy(src, dst, io_sem.at[k])
        for k, (src, dst) in enumerate((
            (sb_hbm, sb_ref), (bs_hbm, bs_ref), (sol_hbm, sol_ref), (mask_hbm, mask_ref), (pop_hbm, out_pop)))
    ]
    for load in loads:
        load.start()
    me = tuple(lax.axis_index(a) for a in AXES)
    lane = iota(1)
    row = iota(0)
    size_z = mask_ref.shape[0] // 16
    slots = sb_ref.shape[0]
    tiles = bs_ref.shape[2]
    comps = sol_ref.shape[0]

    def rows_of(z):
        return pl.ds(z * 16 if isinstance(z, int) else pl.multiple_of(z * 16, 16), 16)

    def exists(off):
        ok = None
        for pos, n, o in zip(me, sizes, off):
            if o == 0:
                continue
            c = (pos + o < n) if o > 0 else (pos >= 1)
            ok = c if ok is None else jnp.logical_and(ok, c)
        return ok

    def dev(off):
        return {a: p + o for a, p, o in zip(AXES, me, off)}

    neighbours = [c for c in FLOW_DIRS[1:]]

    XH[0] = jnp.zeros_like(XH[0])
    YH[0] = jnp.zeros_like(YH[0])
    YE[0] = jnp.zeros_like(YE[0])
    ZH[0] = jnp.zeros_like(ZH[0])

    barrier = pltpu.get_barrier_semaphore()
    count = jnp.int32(n_z - 1)
    for off in neighbours:
        if off[0] == 0 and off[1] == 0:
            continue
        ok = exists(off)
        count = count + ok.astype(jnp.int32)

        @pl.when(ok)
        def _(off=off):
            pl.semaphore_signal(barrier, inc=1, device_id=dev(off), device_id_type=pl.DeviceIdType.MESH)

    for k in range(1, n_z):
        other = lax.rem(me[2] + k, n_z)
        pl.semaphore_signal(
            barrier, inc=1, device_id={"gx": me[0], "gy": me[1], "gz": other},
            device_id_type=pl.DeviceIdType.MESH)

    def routing(values, per):
        group = [lax.div(jnp.maximum(v, 0), jnp.int32(per)) for v in values]
        held = [(v >= 0).astype(jnp.int32) for v in values]
        rank = []
        for s in range(len(values)):
            r = jnp.int32(0)
            for e in range(s):
                r = r + jnp.where(group[e] == group[s], held[e], 0)
            rank.append(r)
        pick = []
        for g in range(n_z):
            for p in range(cap):
                at = jnp.int32(0)
                for s in range(len(values)):
                    hit = jnp.logical_and(group[s] == g, rank[s] == p)
                    at = at + jnp.where(hit, held[s] * s, 0)
                pick.append(at)
        where = [(group[s] * cap + rank[s] + 1) * held[s] - 1 for s in range(len(values))]
        return pick, where

    loads[0].wait()
    loads[1].wait()
    slot_pick, slot_where = routing([sb_ref[s] for s in range(slots)], tiles)
    tile_pick, tile_where = routing([bs_ref[0, 0, j] for j in range(tiles)], slots)
    rows = T.shape[1] // slots

    def blocks_of(c, n):
        return [T[c, k * rows:(k + 1) * rows, :] for k in range(n)]

    def pairs_of(buf, c):
        return [buf[q // cap, q % cap, c] for q in range(n_z * cap)]

    def choose(index, options):
        at = jnp.full(options[0].shape, index, jnp.int32)
        out = jnp.zeros_like(options[0])
        for k, v in enumerate(options):
            out = jnp.where(at == k, v, out)
        return out

    def gather(c, _):
        for r in range(rows):
            T[c, pl.ds(r, slots, stride=rows), :] = sol_ref[c, :, r * 128:(r + 1) * 128]
        for q in range(n_z * cap):
            stage[q // cap, q % cap, c] = choose(slot_pick[q], blocks_of(c, slots))
        return 0

    loads[2].wait()
    lax.fori_loop(0, comps, gather, 0)
    pl.semaphore_wait(barrier, count)

    hops = sorted(range(1, n_z), key=lambda k: abs(2 * k - n_z))

    def block_copies(src, dst, send, rec, own):
        copies = []
        for k in hops:
            other = lax.rem(me[2] + k, n_z)
            copies.append(pltpu.make_async_remote_copy(
                src_ref=src.at[other], dst_ref=dst.at[me[2]],
                send_sem=send.at[k], recv_sem=rec.at[k],
                device_id={"gx": me[0], "gy": me[1], "gz": other},
                device_id_type=pl.DeviceIdType.MESH))
        copies.append(pltpu.make_async_copy(src.at[me[2]], dst.at[me[2]], own))
        return copies

    there = block_copies(stage, recv, a_send, a_recv, own_sem.at[0])
    back = block_copies(stage2, recv2, b_send, b_recv, own_sem.at[1])
    for copy in there:
        copy.start()

    def flow_messages(slot):
        out = []
        for si, s in enumerate(SIGNS):
            for m, (oy, oz) in enumerate(X_OFFS):
                out.append(((s, oy, oz), XM.at[si], XH.at[slot, si, m]))
        for si, s in enumerate(SIGNS):
            out.append(((0, s, 0), YM.at[si], YH.at[slot, si]))
            for zi, z in enumerate(SIGNS):
                src = YM.at[si, 3 + zi, pl.ds(size_z - 8 if z > 0 else 0, 8)]
                out.append(((0, s, z), src, YE.at[slot, si, zi]))
        for si, s in enumerate(SIGNS):
            out.append(((0, 0, s), ZM.at[si], ZH.at[slot, si]))
        return out

    def solute_messages():
        out = []
        for ax in range(3):
            for si, s in enumerate(SIGNS):
                off = tuple(s if a == ax else 0 for a in range(3))
                out.append((off, SM.at[ax, si], SH.at[ax, si]))
        return out

    def exchange(messages, send, rec):
        copies = [
            pltpu.make_async_remote_copy(
                src_ref=src, dst_ref=dst, send_sem=send.at[k], recv_sem=rec(k),
                device_id=dev(off), device_id_type=pl.DeviceIdType.MESH)
            for k, (off, src, dst) in enumerate(messages)
        ]

        def start(which):
            for (off, _, _), copy in zip(messages, copies):
                if which(off):
                    @pl.when(exists(off))
                    def _(copy=copy):
                        copy.start()

        def finish():
            for (off, _, _), copy in zip(messages, copies):
                @pl.when(exists(tuple(-o for o in off)))
                def _(copy=copy):
                    copy.wait_recv()
            for (off, _, _), copy in zip(messages, copies):
                @pl.when(exists(off))
                def _(copy=copy):
                    copy.wait_send()
        return start, finish

    def z_face(off):
        return off[0] == 0 and off[1] == 0

    def not_z_face(off):
        return not z_face(off)

    def pack_x(z, planes, acc):
        new = []
        at_z = (lane & 15) == z
        for si, s in enumerate(SIGNS):
            w = None
            for j, v in enumerate(planes[si]):
                r = pltpu.roll(v, z + (16 * j + 1 if s > 0 else 16 * j), 1)
                w = r if w is None else jnp.where((lane >= 16 * j), r, w)
            new.append(jnp.where(at_z, w, acc[si]))
        return tuple(new)

    def pack_flow(z, values, acc):
        for si, s in enumerate(SIGNS):
            e = 15 if s > 0 else 0
            for j, d in enumerate(Y_SIDE[si]):
                YM[si, j, pl.ds(z, 1), :] = values[d][e:e + 1, :]
        return pack_x(z, [[values[d] for d in X_SIDE[si]] for si in range(2)], acc)

    def z_pack():
        for si, s in enumerate(SIGNS):
            for j, d in enumerate(Z_SIDE[si]):
                ZM[si, j] = F[d, size_z if s > 0 else 1]

    zero2 = (jnp.zeros((16, 128), jnp.float32),) * 2

    def z_halo(slot):
        for si, s in enumerate(SIGNS):
            for j, d in enumerate(Z_SIDE[si]):
                F[d, 0 if s > 0 else size_z + 1] = ZH[slot, si, j]

    def flow_halo(slot):
        for si, s in enumerate(SIGNS):
            for zi, z in enumerate(SIGNS):
                base = YH[slot, si, 3 + zi]
                e = YE[slot, si, zi, 7:8, :] if z > 0 else YE[slot, si, zi, 0:1, :]
                edge = row == (15 if z > 0 else 0)
                YC[si, zi] = pltpu.roll(jnp.where(edge, jnp.broadcast_to(e, (16, 128)), base), 1 if z > 0 else 15, 0)
            base = XH[slot, si, 0]
            g1 = pltpu.roll(jnp.where(row == 15, XH[slot, si, 1], base), 1, 0)
            g2 = pltpu.roll(jnp.where(row == 0, XH[slot, si, 2], base), 15, 0)
            g3 = jnp.where(lane == 48, pltpu.roll(XH[slot, si, 3], 113, 1), pltpu.roll(base, 1, 1))
            g4 = jnp.where(lane == 79, pltpu.roll(XH[slot, si, 4], 15, 1), pltpu.roll(base, 127, 1))
            c = jnp.where(lane < 16, base, g1)
            c = jnp.where(lane < 32, c, g2)
            c = jnp.where(lane < 48, c, g3)
            XC[si] = jnp.where(lane < 64, c, g4)

    def shifted_flow(slot, z, xz):
        out = [None]
        for d in range(1, 19):
            cx, cy, cz = FLOW_DIRS[d]
            v = F[d, z + (1 - cz)]
            if cy:
                si = side(cy)
                j = Y_SIDE[si].index(d)
                if j < 3:
                    e = YH[slot, si, j, pl.ds(z, 1), :]
                else:
                    e = YC[si, j - 3, pl.ds(z, 1), :]
                v = jnp.where(row == (0 if cy > 0 else 15), jnp.broadcast_to(e, (16, 128)),
                              pltpu.roll(v, 1 if cy > 0 else 15, 0))
            if cx:
                si = side(cx)
                j = X_SIDE[si].index(d)
                if cx > 0:
                    h = pltpu.roll(xz[0], (128 - 16 * j) - z if j else lax.rem(128 - z, 128), 1)
                    v = jnp.where(lane == 0, h, pltpu.roll(v, 1, 1))
                else:
                    h = pltpu.roll(xz[1], (127 - 16 * j) - z, 1)
                    v = jnp.where(lane == 127, h, pltpu.roll(v, 127, 1))
            out.append(v)
        return out

    def moments(z, p, porous):
        density = p[0]
        for v in p[1:]:
            density = density + v
        inv = porous / density
        m = []
        for ax in range(3):
            total = None
            for d in range(1, 19):
                if FLOW_DIRS[d][ax] > 0:
                    diff = p[d] - p[OPP[d]]
                    total = diff if total is None else total + diff
            m.append(total * inv)
        U[0, z] = density
        for ax in range(3):
            U[1 + ax, z] = m[ax]

    loads[3].wait()
    loads[4].wait()

    def fill(z, acc):
        porous = mask_ref[rows_of(z), :].astype(jnp.float32)
        for d in range(19):
            F[d, z + 1] = porous
        moments(z, [out_pop[d, rows_of(z), :] for d in range(19)], porous)
        return pack_flow(z, [porous] * 19, acc)

    XM[0], XM[1] = planes_loop(size_z, fill, zero2)
    z_pack()
    start, finish = exchange(flow_messages(0), f_send, lambda k: f_recv.at[0, k])
    start(lambda off: True)
    finish()
    z_halo(0)
    flow_halo(0)

    def link_bits(z, _):
        xz = [XC[0], XC[1]]
        moved = shifted_flow(0, z, xz)
        pore = mask_ref[rows_of(z), :] > 0
        bits = jnp.where(pore, 1, 0)
        for d in range(1, 19):
            bits = bits | jnp.where(jnp.logical_and(pore, moved[d] > 0.5), 1 << d, 0)
        B[rows_of(z), :] = bits
        return 0

    planes_loop(size_z, link_bits, 0)

    for copy in there:
        copy.wait()

    def place(c, _):
        for j in range(tiles):
            T[c, j * rows:(j + 1) * rows, :] = choose(tile_where[j], pairs_of(recv, c))
        for r in range(rows):
            v = T[c, pl.ds(r, tiles, stride=rows), :]
            G[c, r // 2, (r % 2) * 8:(r % 2) * 8 + 8, :] = swap_chunks(v)
        return 0

    lax.fori_loop(0, comps, place, 0)

    def unplace(c, _):
        for r in range(rows):
            T[c, pl.ds(r, tiles, stride=rows), :] = swap_chunks(G[c, r // 2, (r % 2) * 8:(r % 2) * 8 + 8, :])
        for q in range(n_z * cap):
            stage2[q // cap, q % cap, c] = choose(tile_pick[q], blocks_of(c, tiles))
        return 0

    def collide_solute(z, acc):
        g = [G[i, z] for i in range(7)]
        u = [U[1 + a, z] for a in range(3)]
        conc = g[0]
        for v in g[1:]:
            conc = conc + v
        post = [g[0] * (1 - OMEGA_SOLUTE) + (OMEGA_SOLUTE * 0.25) * conc]
        cw = (OMEGA_SOLUTE * 0.125) * conc
        for i in range(1, 7):
            ax = (i - 1) // 2
            f = 1.0 + 4.0 * u[ax] if i % 2 else 1.0 - 4.0 * u[ax]
            post.append(g[i] * (1 - OMEGA_SOLUTE) + cw * f)
        for i in range(7):
            S[i, z + 1] = post[i]
        SM[1, 0, pl.ds(z, 1), :] = post[3][15:16, :]
        SM[1, 1, pl.ds(z, 1), :] = post[4][0:1, :]
        at_z = lane == z
        return (jnp.where(at_z, pltpu.roll(post[1], z + 1, 1), acc[0]),
                jnp.where(at_z, pltpu.roll(post[2], z, 1), acc[1]))

    def stream_solute(z, acc):
        bits = B[rows_of(z), :]
        pore = (bits & 1) != 0
        xz = [SH[0, 0], SH[0, 1]]
        s = [S[i, z + 1] for i in range(7)]
        new = [s[0]]
        for i in range(1, 7):
            cx, cy, cz = FLOW_DIRS[i]
            if cx > 0:
                v = jnp.where(lane == 0, pltpu.roll(xz[0], lax.rem(128 - z, 128), 1), pltpu.roll(s[i], 1, 1))
            elif cx < 0:
                v = jnp.where(lane == 127, pltpu.roll(xz[1], 127 - z, 1), pltpu.roll(s[i], 127, 1))
            elif cy:
                e = SH[1, side(cy), pl.ds(z, 1), :]
                v = jnp.where(row == (0 if cy > 0 else 15), jnp.broadcast_to(e, (16, 128)),
                              pltpu.roll(s[i], 1 if cy > 0 else 15, 0))
            else:
                v = S[i, z + (1 - cz)]
            new.append(jnp.where((bits & (1 << i)) != 0, v, jnp.where(pore, s[OPP[i]], s[i])))
        for i in range(7):
            G[i, z] = new[i]
        return new

    def collide_flow(z, acc, new):
        pore = (B[rows_of(z), :] & 1) != 0
        conc = new[0]
        for v in new[1:]:
            conc = conc + v
        rho = U[0, z]
        ux = U[1, z]
        uy = U[2, z]
        uz = U[3, z] + jnp.where(pore, FORCE_GAIN * (conc - REST_CONC), 0.0)
        base = 1.0 - 1.5 * (ux * ux + uy * uy + uz * uz)
        p = [out_pop[d, rows_of(z), :] for d in range(19)]
        post = [None] * 19
        post[0] = jnp.where(pore, p[0] * (1 - OMEGA_FLOW) + (OMEGA_FLOW / 3.0) * rho * base, p[0])
        w1 = (OMEGA_FLOW / 18.0) * rho
        w2 = (OMEGA_FLOW / 36.0) * rho
        for d in range(1, 19, 2):
            o = OPP[d]
            along = None
            for c, u in zip(FLOW_DIRS[d], (ux, uy, uz)):
                if c:
                    along = (u if c > 0 else -u) if along is None else (along + u if c > 0 else along - u)
            w = w1 if d < 7 else w2
            even = base + 4.5 * along * along
            odd = 3.0 * along
            post[d] = jnp.where(pore, p[d] * (1 - OMEGA_FLOW) + w * (even + odd), p[d])
            post[o] = jnp.where(pore, p[o] * (1 - OMEGA_FLOW) + w * (even - odd), p[o])
        for d in range(19):
            F[d, z + 1] = post[d]
        return pack_flow(z, post, acc)

    def shift_in_plane(d, v):
        cx, cy, _ = FLOW_DIRS[d]
        if cy:
            v = pltpu.roll(v, 1 if cy > 0 else 15, 0)
        if cx:
            v = pltpu.roll(v, 1 if cx > 0 else 127, 1)
        return v

    def stream_inside(z, _):
        bits = B[rows_of(z), :]
        pore = (bits & 1) != 0
        here = [F[d, z + 1] for d in range(19)]
        out_pop[0, rows_of(z), :] = here[0]
        for d in range(1, 19):
            cz = FLOW_DIRS[d][2]
            v = shift_in_plane(d, F[d, z + (1 - cz)] if cz else here[d])
            out_pop[d, rows_of(z), :] = jnp.where(
                (bits & (1 << d)) != 0, v, jnp.where(pore, here[OPP[d]], here[d]))
        return 0

    def edges_yz(slot):
        for si, s in enumerate(SIGNS):
            z = 0 if s > 0 else size_z - 1
            bits = B[rows_of(z), :]
            for j, d in enumerate(Z_SIDE[si]):
                v = shift_in_plane(d, ZH[slot, si, j])
                out_pop[d, rows_of(z), :] = jnp.where((bits & (1 << d)) != 0, v, out_pop[d, rows_of(z), :])
        for si, s in enumerate(SIGNS):
            at = pl.ds(0 if s > 0 else 15, size_z, stride=16)
            bits = B[at, :]
            for j, d in enumerate(Y_SIDE[si]):
                cx = FLOW_DIRS[d][0]
                v = YH[slot, si, j] if j < 3 else YC[si, j - 3]
                if cx:
                    v = pltpu.roll(v, 1 if cx > 0 else 127, 1)
                out_pop[d, at, :] = jnp.where((bits & (1 << d)) != 0, v, out_pop[d, at, :])

    def edge_x(z):
        bits = B[rows_of(z), :]
        p = [out_pop[d, rows_of(z), :] for d in range(19)]
        for si, s in enumerate(SIGNS):
            edge = jnp.where(lane == (0 if s > 0 else 127), bits, 0)
            for j, d in enumerate(X_SIDE[si]):
                back = (128 if s > 0 else 127) - 16 * j - z
                if s > 0 and j == 0:
                    back = lax.rem(back, 128)
                p[d] = jnp.where((edge & (1 << d)) != 0, pltpu.roll(XC[si], back, 1), p[d])
                out_pop[d, rows_of(z), :] = p[d]
        return p, bits

    def edge_x_collide(z, acc):
        p, bits = edge_x(z)
        moments(z, p, jnp.where((bits & 1) != 0, 1.0, 0.0))
        return collide_solute(z, acc)

    def solute_post(body):
        SM[0, 0], SM[0, 1] = planes_loop(size_z, body, zero2)
        for si in range(2):
            SM[2, si] = S[5 + si, size_z if si == 0 else 1]

    def step(t, last):
        slot = lax.rem(t + 1, 2)
        start, finish = exchange(solute_messages(), s_send, lambda k: s_recv.at[k])
        start(lambda off: True)
        finish()
        S[5, 0] = SH[2, 0]
        S[6, size_z + 1] = SH[2, 1]

        def collide(z, acc):
            return collide_flow(z, acc, stream_solute(z, None))

        XM[0], XM[1] = planes_loop(size_z, collide, zero2)
        z_pack()
        start, finish = exchange(flow_messages(slot), f_send, lambda k: f_recv.at[slot, k])
        start(z_face)
        start(not_z_face)
        if last:
            lax.fori_loop(0, comps, unplace, 0)
            for copy in back:
                copy.start()
        planes_loop(size_z, stream_inside, 0)
        finish()
        flow_halo(slot)
        edges_yz(slot)
        if last:
            planes_loop(size_z, lambda z, _: (edge_x(z), 0)[1], 0)
        else:
            solute_post(edge_x_collide)

    solute_post(collide_solute)
    lax.fori_loop(0, STEPS - 1, lambda t, _: (step(t, False), 0)[1], 0)
    step(jnp.int32(STEPS - 1), True)
    store_pop = pltpu.make_async_copy(out_pop, pop_out, io_sem.at[5])
    store_pop.start()

    for copy in back:
        copy.wait()

    def deliver(c, _):
        for s in range(slots):
            T[c, s * rows:(s + 1) * rows, :] = choose(slot_where[s], pairs_of(recv2, c))
        for r in range(rows):
            out_sol[c, :, r * 128:(r + 1) * 128] = T[c, pl.ds(r, slots, stride=rows), :]
        pltpu.make_async_copy(out_sol.at[c], sol_out.at[c], sol_sem.at[c]).start()
        return 0

    lax.fori_loop(0, comps, deliver, 0)
    for c in range(comps):
        pltpu.make_async_copy(out_sol.at[c], sol_out.at[c], sol_sem.at[c]).wait()
    store_pop.wait()


def shards(sizes, populations, solute_state, pore_mask, block_slot, slot_block):
    n_z = sizes[2]
    tiles = block_slot.shape[2]
    cap = -(-tiles // n_z)
    comps, slots, cells = solute_state.shape
    rows = cells // 128
    sz, sy, sx = pore_mask.shape
    f32 = jnp.float32
    blocks = pltpu.VMEM((n_z, cap, comps, rows, 128), f32)
    dma = pltpu.SemaphoreType.DMA
    hbm = pl.BlockSpec(memory_space=pl.ANY)
    new_populations, new_solute = pl.pallas_call(
        functools.partial(kernel, sizes, cap),
        out_shape=(
            jax.ShapeDtypeStruct((19, sz * sy, sx), f32),
            jax.ShapeDtypeStruct(solute_state.shape, f32),
        ),
        in_specs=[hbm] * 5,
        out_specs=(hbm, hbm),
        scratch_shapes=[
            pltpu.VMEM((19, sz * sy, sx), f32),
            pltpu.VMEM(solute_state.shape, f32),
            pltpu.VMEM(solute_state.shape, f32),
            pltpu.VMEM((sz * sy, sx), jnp.int32),
            pltpu.SMEM(block_slot.shape, jnp.int32),
            pltpu.SMEM(slot_block.shape, jnp.int32),
            pltpu.VMEM((19, sz + 2, sy, sx), f32),
            pltpu.VMEM((7, sz, sy, sx), f32),
            pltpu.VMEM((7, sz + 2, sy, sx), f32),
            pltpu.VMEM((4, sz, sy, sx), f32),
            pltpu.VMEM((sz * sy, sx), jnp.int32),
            pltpu.VMEM((2, 16, 128), f32),
            pltpu.VMEM((2, 5, 16, 128), f32),
            pltpu.VMEM((2, 5, 16, 128), f32),
            pltpu.VMEM((2, 2, 5, 16, 128), f32),
            pltpu.VMEM((2, 2, 5, 16, 128), f32),
            pltpu.VMEM((2, 2, 2, 8, 128), f32),
            pltpu.VMEM((2, 2, 5, 16, 128), f32),
            pltpu.VMEM((2, 16, 128), f32),
            pltpu.VMEM((2, 2, 16, 128), f32),
            pltpu.VMEM((3, 2, 16, 128), f32),
            pltpu.VMEM((3, 2, 16, 128), f32),
            pltpu.VMEM((comps, slots * rows, 128), f32),
            blocks, blocks, blocks, blocks,
            dma((18,)), dma((2, 18)), dma((6,)), dma((6,)),
            dma((n_z,)), dma((n_z,)), dma((n_z,)), dma((n_z,)), dma((2,)), dma((6,)), dma((comps,)),
        ],
        compiler_params=pltpu.CompilerParams(
            collective_id=0, has_side_effects=True, vmem_limit_bytes=56 * 1024 * 1024),
    )(populations.reshape(19, sz * sy, sx), solute_state, pore_mask.reshape(sz * sy, sx), block_slot, slot_block)
    return new_populations.reshape(populations.shape), new_solute


def solution(mesh):
    sizes = tuple(mesh.shape[a] for a in AXES)
    in_specs = (
        P(None, "gz", "gy", "gx"),
        P(None, ("gx", "gy", "gz"), None),
        P("gz", "gy", "gx"),
        P("gz", "gy", "gx"),
        P(("gx", "gy", "gz")),
    )
    out_specs = (P(None, "gz", "gy", "gx"), P(None, ("gx", "gy", "gz"), None))
    return jax.shard_map(
        functools.partial(shards, sizes), mesh=mesh, in_specs=in_specs, out_specs=out_specs, check_vma=False)
```

```python
import functools

import jax
import jax.numpy as jnp
from jax import lax
from jax.experimental import pallas as pl
from jax.experimental.pallas import tpu as pltpu
from jax.sharding import PartitionSpec as P

STEPS = 4
AXES = ("gx", "gy", "gz")

FLOW_DIRS = [
    (0, 0, 0),
    (1, 0, 0),
    (-1, 0, 0),
    (0, 1, 0),
    (0, -1, 0),
    (0, 0, 1),
    (0, 0, -1),
    (1, 1, 0),
    (-1, -1, 0),
    (1, -1, 0),
    (-1, 1, 0),
    (1, 0, 1),
    (-1, 0, -1),
    (1, 0, -1),
    (-1, 0, 1),
    (0, 1, 1),
    (0, -1, -1),
    (0, 1, -1),
    (0, -1, 1),
]
FLOW_WEIGHTS = [1.0 / 3.0] + [1.0 / 18.0] * 6 + [1.0 / 36.0] * 12
OPP = [FLOW_DIRS.index((-a, -b, -c)) for a, b, c in FLOW_DIRS]
OMEGA_FLOW = 1.2
OMEGA_SOLUTE = 1.5
FORCE_GAIN = 0.02
REST_CONC = 8.0
SIGNS = (1, -1)

X_SIDE = [[FLOW_DIRS.index((s, b, c)) for b, c in ((0, 0), (1, 0), (-1, 0), (0, 1), (0, -1))] for s in SIGNS]
Y_SIDE = [[FLOW_DIRS.index((a, s, c)) for a, c in ((0, 0), (1, 0), (-1, 0), (0, 1), (0, -1))] for s in SIGNS]
Z_SIDE = [[FLOW_DIRS.index((a, b, s)) for a, b in ((0, 0), (1, 0), (-1, 0), (0, 1), (0, -1))] for s in SIGNS]
X_OFFS = [(0, 0), (1, 0), (-1, 0), (0, 1), (0, -1)]


def side(sign):
    return 0 if sign > 0 else 1


def planes_loop(n, body, init, first=0, unroll=4):
    def group(g, acc):
        for k in range(unroll):
            acc = body(first + g * unroll + k, acc)
        return acc
    return lax.fori_loop(0, n // unroll, group, init)


def iota(axis, shape=(16, 128)):
    return lax.broadcasted_iota(jnp.int32, shape, axis)


def swap_chunks(v):
    sub = iota(0, (8, 128))
    chunk = lax.shift_right_logical(iota(1, (8, 128)), 4)
    for k in (1, 2, 4):
        sbit = (sub & k) != 0
        if k == 4:
            both = pltpu.roll(pltpu.roll(v, 64, 1), 4, 0)
            v = jnp.where(((sub ^ chunk) & k) == 0, v, both)
        else:
            up = pltpu.roll(pltpu.roll(v, 16 * k, 1), 8 - k, 0)
            down = pltpu.roll(pltpu.roll(v, 128 - 16 * k, 1), k, 0)
            same = ((sub ^ chunk) & k) == 0
            v = jnp.where(same, v, jnp.where(sbit, down, up))
    return v


def kernel(
    sizes, cap, pop_hbm, sol_hbm, mask_hbm, bs_hbm, sb_hbm, pop_out, sol_out,
    out_pop, out_sol, sol_ref, mask_ref, bs_ref, sb_ref,
    F, G, S, U, B, XM, YM, ZM, XH, YH, YE, ZH, XC, YC, SM, SH,
    T, stage, recv, stage2, recv2,
    f_send, f_recv, s_send, s_recv, a_send, a_recv, b_send, b_recv, own_sem, io_sem, sol_sem,
):
    n_x, n_y, n_z = sizes
    loads = [
        pltpu.make_async_copy(src, dst, io_sem.at[k])
        for k, (src, dst) in enumerate((
            (sb_hbm, sb_ref), (bs_hbm, bs_ref), (sol_hbm, sol_ref), (mask_hbm, mask_ref), (pop_hbm, out_pop)))
    ]
    for load in loads:
        load.start()
    me = tuple(lax.axis_index(a) for a in AXES)
    lane = iota(1)
    row = iota(0)
    size_z = mask_ref.shape[0] // 16
    slots = sb_ref.shape[0]
    tiles = bs_ref.shape[2]
    comps = sol_ref.shape[0]

    def rows_of(z):
        return pl.ds(z * 16 if isinstance(z, int) else pl.multiple_of(z * 16, 16), 16)

    def exists(off):
        ok = None
        for pos, n, o in zip(me, sizes, off):
            if o == 0:
                continue
            c = (pos + o < n) if o > 0 else (pos >= 1)
            ok = c if ok is None else jnp.logical_and(ok, c)
        return ok

    def dev(off):
        return {a: p + o for a, p, o in zip(AXES, me, off)}

    neighbours = [c for c in FLOW_DIRS[1:]]

    XH[0] = jnp.zeros_like(XH[0])
    YH[0] = jnp.zeros_like(YH[0])
    YE[0] = jnp.zeros_like(YE[0])
    ZH[0] = jnp.zeros_like(ZH[0])

    barrier = pltpu.get_barrier_semaphore()
    count = jnp.int32(n_z - 1)
    for off in neighbours:
        if off[0] == 0 and off[1] == 0:
            continue
        ok = exists(off)
        count = count + ok.astype(jnp.int32)

        @pl.when(ok)
        def _(off=off):
            pl.semaphore_signal(barrier, inc=1, device_id=dev(off), device_id_type=pl.DeviceIdType.MESH)

    for k in range(1, n_z):
        other = lax.rem(me[2] + k, n_z)
        pl.semaphore_signal(
            barrier, inc=1, device_id={"gx": me[0], "gy": me[1], "gz": other},
            device_id_type=pl.DeviceIdType.MESH)

    def routing(values, per):
        group = [lax.div(jnp.maximum(v, 0), jnp.int32(per)) for v in values]
        held = [(v >= 0).astype(jnp.int32) for v in values]
        rank = []
        for s in range(len(values)):
            r = jnp.int32(0)
            for e in range(s):
                r = r + jnp.where(group[e] == group[s], held[e], 0)
            rank.append(r)
        pick = []
        for g in range(n_z):
            for p in range(cap):
                at = jnp.int32(0)
                for s in range(len(values)):
                    hit = jnp.logical_and(group[s] == g, rank[s] == p)
                    at = at + jnp.where(hit, held[s] * s, 0)
                pick.append(at)
        where = [(group[s] * cap + rank[s] + 1) * held[s] - 1 for s in range(len(values))]
        return pick, where

    loads[0].wait()
    loads[1].wait()
    slot_pick, slot_where = routing([sb_ref[s] for s in range(slots)], tiles)
    tile_pick, tile_where = routing([bs_ref[0, 0, j] for j in range(tiles)], slots)
    rows = T.shape[1] // slots

    def blocks_of(c, n):
        return [T[c, k * rows:(k + 1) * rows, :] for k in range(n)]

    def pairs_of(buf, c):
        return [buf[q // cap, q % cap, c] for q in range(n_z * cap)]

    def choose(index, options):
        at = jnp.full(options[0].shape, index, jnp.int32)
        out = jnp.zeros_like(options[0])
        for k, v in enumerate(options):
            out = jnp.where(at == k, v, out)
        return out

    def gather(c, _):
        for r in range(rows):
            T[c, pl.ds(r, slots, stride=rows), :] = sol_ref[c, :, r * 128:(r + 1) * 128]
        for q in range(n_z * cap):
            stage[q // cap, q % cap, c] = choose(slot_pick[q], blocks_of(c, slots))
        return 0

    loads[2].wait()
    lax.fori_loop(0, comps, gather, 0)

    hops = sorted(range(1, n_z), key=lambda k: abs(2 * k - n_z))

    def block_copies(src, dst, send, rec, own):
        copies = []
        for k in hops:
            other = lax.rem(me[2] + k, n_z)
            copies.append(pltpu.make_async_remote_copy(
                src_ref=src.at[other], dst_ref=dst.at[me[2]],
                send_sem=send.at[k], recv_sem=rec.at[k],
                device_id={"gx": me[0], "gy": me[1], "gz": other},
                device_id_type=pl.DeviceIdType.MESH))
        copies.append(pltpu.make_async_copy(src.at[me[2]], dst.at[me[2]], own))
        return copies

    there = block_copies(stage, recv, a_send, a_recv, own_sem.at[0])
    back = block_copies(stage2, recv2, b_send, b_recv, own_sem.at[1])
    def flow_messages(slot):
        out = []
        for si, s in enumerate(SIGNS):
            for m, (oy, oz) in enumerate(X_OFFS):
                out.append(((s, oy, oz), XM.at[si], XH.at[slot, si, m]))
        for si, s in enumerate(SIGNS):
            out.append(((0, s, 0), YM.at[si], YH.at[slot, si]))
            for zi, z in enumerate(SIGNS):
                src = YM.at[si, 3 + zi, pl.ds(size_z - 8 if z > 0 else 0, 8)]
                out.append(((0, s, z), src, YE.at[slot, si, zi]))
        for si, s in enumerate(SIGNS):
            out.append(((0, 0, s), ZM.at[si], ZH.at[slot, si]))
        return out

    def solute_messages():
        out = []
        for ax in range(3):
            for si, s in enumerate(SIGNS):
                off = tuple(s if a == ax else 0 for a in range(3))
                out.append((off, SM.at[ax, si], SH.at[ax, si]))
        return out

    def exchange(messages, send, rec):
        copies = [
            pltpu.make_async_remote_copy(
                src_ref=src, dst_ref=dst, send_sem=send.at[k], recv_sem=rec(k),
                device_id=dev(off), device_id_type=pl.DeviceIdType.MESH)
            for k, (off, src, dst) in enumerate(messages)
        ]

        def start(which):
            for (off, _, _), copy in zip(messages, copies):
                if which(off):
                    @pl.when(exists(off))
                    def _(copy=copy):
                        copy.start()

        def finish():
            for (off, _, _), copy in zip(messages, copies):
                @pl.when(exists(tuple(-o for o in off)))
                def _(copy=copy):
                    copy.wait_recv()
            for (off, _, _), copy in zip(messages, copies):
                @pl.when(exists(off))
                def _(copy=copy):
                    copy.wait_send()
        return start, finish

    def z_face(off):
        return off[0] == 0 and off[1] == 0

    def not_z_face(off):
        return not z_face(off)

    def pack_x(z, planes, acc):
        new = []
        at_z = (lane & 15) == z
        for si, s in enumerate(SIGNS):
            w = None
            for j, v in enumerate(planes[si]):
                r = pltpu.roll(v, z + (16 * j + 1 if s > 0 else 16 * j), 1)
                w = r if w is None else jnp.where((lane >= 16 * j), r, w)
            new.append(jnp.where(at_z, w, acc[si]))
        return tuple(new)

    def pack_flow(z, values, acc):
        for si, s in enumerate(SIGNS):
            e = 15 if s > 0 else 0
            for j, d in enumerate(Y_SIDE[si]):
                YM[si, j, pl.ds(z, 1), :] = values[d][e:e + 1, :]
        return pack_x(z, [[values[d] for d in X_SIDE[si]] for si in range(2)], acc)

    def z_pack():
        for si, s in enumerate(SIGNS):
            for j, d in enumerate(Z_SIDE[si]):
                ZM[si, j] = F[d, size_z if s > 0 else 1]

    zero2 = (jnp.zeros((16, 128), jnp.float32),) * 2

    def z_halo(slot):
        for si, s in enumerate(SIGNS):
            for j, d in enumerate(Z_SIDE[si]):
                F[d, 0 if s > 0 else size_z + 1] = ZH[slot, si, j]

    def flow_halo(slot):
        for si, s in enumerate(SIGNS):
            for zi, z in enumerate(SIGNS):
                base = YH[slot, si, 3 + zi]
                e = YE[slot, si, zi, 7:8, :] if z > 0 else YE[slot, si, zi, 0:1, :]
                edge = row == (15 if z > 0 else 0)
                YC[si, zi] = pltpu.roll(jnp.where(edge, jnp.broadcast_to(e, (16, 128)), base), 1 if z > 0 else 15, 0)
            base = XH[slot, si, 0]
            g1 = pltpu.roll(jnp.where(row == 15, XH[slot, si, 1], base), 1, 0)
            g2 = pltpu.roll(jnp.where(row == 0, XH[slot, si, 2], base), 15, 0)
            g3 = jnp.where(lane == 48, pltpu.roll(XH[slot, si, 3], 113, 1), pltpu.roll(base, 1, 1))
            g4 = jnp.where(lane == 79, pltpu.roll(XH[slot, si, 4], 15, 1), pltpu.roll(base, 127, 1))
            c = jnp.where(lane < 16, base, g1)
            c = jnp.where(lane < 32, c, g2)
            c = jnp.where(lane < 48, c, g3)
            XC[si] = jnp.where(lane < 64, c, g4)

    def shifted_flow(slot, z, xz):
        out = [None]
        for d in range(1, 19):
            cx, cy, cz = FLOW_DIRS[d]
            v = F[d, z + (1 - cz)]
            if cy:
                si = side(cy)
                j = Y_SIDE[si].index(d)
                if j < 3:
                    e = YH[slot, si, j, pl.ds(z, 1), :]
                else:
                    e = YC[si, j - 3, pl.ds(z, 1), :]
                v = jnp.where(row == (0 if cy > 0 else 15), jnp.broadcast_to(e, (16, 128)),
                              pltpu.roll(v, 1 if cy > 0 else 15, 0))
            if cx:
                si = side(cx)
                j = X_SIDE[si].index(d)
                if cx > 0:
                    h = pltpu.roll(xz[0], (128 - 16 * j) - z if j else lax.rem(128 - z, 128), 1)
                    v = jnp.where(lane == 0, h, pltpu.roll(v, 1, 1))
                else:
                    h = pltpu.roll(xz[1], (127 - 16 * j) - z, 1)
                    v = jnp.where(lane == 127, h, pltpu.roll(v, 127, 1))
            out.append(v)
        return out

    def moments(z, p, porous):
        density = p[0]
        for v in p[1:]:
            density = density + v
        inv = porous / density
        m = []
        for ax in range(3):
            total = None
            for d in range(1, 19):
                if FLOW_DIRS[d][ax] > 0:
                    diff = p[d] - p[OPP[d]]
                    total = diff if total is None else total + diff
            m.append(total * inv)
        U[0, z] = density
        for ax in range(3):
            U[1 + ax, z] = m[ax]

    loads[3].wait()

    def fill(z, acc):
        porous = mask_ref[rows_of(z), :].astype(jnp.float32)
        for d in range(19):
            F[d, z + 1] = porous
        return pack_flow(z, [porous] * 19, acc)

    XM[0], XM[1] = planes_loop(size_z, fill, zero2)
    z_pack()
    start, finish = exchange(flow_messages(0), f_send, lambda k: f_recv.at[0, k])
    pl.semaphore_wait(barrier, count)
    start(z_face)
    start(not_z_face)
    for copy in there:
        copy.start()
    loads[4].wait()

    def first_moments(z, _):
        moments(z, [out_pop[d, rows_of(z), :] for d in range(19)], mask_ref[rows_of(z), :].astype(jnp.float32))
        return 0

    planes_loop(size_z, first_moments, 0)
    finish()
    z_halo(0)
    flow_halo(0)

    def link_bits(z, _):
        xz = [XC[0], XC[1]]
        moved = shifted_flow(0, z, xz)
        pore = mask_ref[rows_of(z), :] > 0
        bits = jnp.where(pore, 1, 0)
        for d in range(1, 19):
            bits = bits | jnp.where(jnp.logical_and(pore, moved[d] > 0.5), 1 << d, 0)
        B[rows_of(z), :] = bits
        return 0

    planes_loop(size_z, link_bits, 0)

    for copy in there:
        copy.wait()

    def place(c, _):
        for j in range(tiles):
            T[c, j * rows:(j + 1) * rows, :] = choose(tile_where[j], pairs_of(recv, c))
        for r in range(rows):
            v = T[c, pl.ds(r, tiles, stride=rows), :]
            G[c, r // 2, (r % 2) * 8:(r % 2) * 8 + 8, :] = swap_chunks(v)
        return 0

    lax.fori_loop(0, comps, place, 0)

    def unplace(c, _):
        for r in range(rows):
            T[c, pl.ds(r, tiles, stride=rows), :] = swap_chunks(G[c, r // 2, (r % 2) * 8:(r % 2) * 8 + 8, :])
        for q in range(n_z * cap):
            stage2[q // cap, q % cap, c] = choose(tile_pick[q], blocks_of(c, tiles))
        return 0

    def collide_solute(z, acc):
        g = [G[i, z] for i in range(7)]
        u = [U[1 + a, z] for a in range(3)]
        conc = g[0]
        for v in g[1:]:
            conc = conc + v
        post = [g[0] * (1 - OMEGA_SOLUTE) + (OMEGA_SOLUTE * 0.25) * conc]
        cw = (OMEGA_SOLUTE * 0.125) * conc
        for i in range(1, 7):
            ax = (i - 1) // 2
            f = 1.0 + 4.0 * u[ax] if i % 2 else 1.0 - 4.0 * u[ax]
            post.append(g[i] * (1 - OMEGA_SOLUTE) + cw * f)
        for i in range(7):
            S[i, z + 1] = post[i]
        SM[1, 0, pl.ds(z, 1), :] = post[3][15:16, :]
        SM[1, 1, pl.ds(z, 1), :] = post[4][0:1, :]
        at_z = lane == z
        return (jnp.where(at_z, pltpu.roll(post[1], z + 1, 1), acc[0]),
                jnp.where(at_z, pltpu.roll(post[2], z, 1), acc[1]))

    def stream_solute(z, acc):
        bits = B[rows_of(z), :]
        pore = (bits & 1) != 0
        xz = [SH[0, 0], SH[0, 1]]
        s = [S[i, z + 1] for i in range(7)]
        new = [s[0]]
        for i in range(1, 7):
            cx, cy, cz = FLOW_DIRS[i]
            if cx > 0:
                v = jnp.where(lane == 0, pltpu.roll(xz[0], lax.rem(128 - z, 128), 1), pltpu.roll(s[i], 1, 1))
            elif cx < 0:
                v = jnp.where(lane == 127, pltpu.roll(xz[1], 127 - z, 1), pltpu.roll(s[i], 127, 1))
            elif cy:
                e = SH[1, side(cy), pl.ds(z, 1), :]
                v = jnp.where(row == (0 if cy > 0 else 15), jnp.broadcast_to(e, (16, 128)),
                              pltpu.roll(s[i], 1 if cy > 0 else 15, 0))
            else:
                v = S[i, z + (1 - cz)]
            new.append(jnp.where((bits & (1 << i)) != 0, v, jnp.where(pore, s[OPP[i]], s[i])))
        for i in range(7):
            G[i, z] = new[i]
        return new

    def collide_flow(z, acc, new):
        pore = (B[rows_of(z), :] & 1) != 0
        conc = new[0]
        for v in new[1:]:
            conc = conc + v
        rho = U[0, z]
        ux = U[1, z]
        uy = U[2, z]
        uz = U[3, z] + jnp.where(pore, FORCE_GAIN * (conc - REST_CONC), 0.0)
        base = 1.0 - 1.5 * (ux * ux + uy * uy + uz * uz)
        p = [out_pop[d, rows_of(z), :] for d in range(19)]
        post = [None] * 19
        post[0] = jnp.where(pore, p[0] * (1 - OMEGA_FLOW) + (OMEGA_FLOW / 3.0) * rho * base, p[0])
        w1 = (OMEGA_FLOW / 18.0) * rho
        w2 = (OMEGA_FLOW / 36.0) * rho
        for d in range(1, 19, 2):
            o = OPP[d]
            along = None
            for c, u in zip(FLOW_DIRS[d], (ux, uy, uz)):
                if c:
                    along = (u if c > 0 else -u) if along is None else (along + u if c > 0 else along - u)
            w = w1 if d < 7 else w2
            even = base + 4.5 * along * along
            odd = 3.0 * along
            post[d] = jnp.where(pore, p[d] * (1 - OMEGA_FLOW) + w * (even + odd), p[d])
            post[o] = jnp.where(pore, p[o] * (1 - OMEGA_FLOW) + w * (even - odd), p[o])
        for d in range(19):
            F[d, z + 1] = post[d]
        return pack_flow(z, post, acc)

    def shift_in_plane(d, v):
        cx, cy, _ = FLOW_DIRS[d]
        if cy:
            v = pltpu.roll(v, 1 if cy > 0 else 15, 0)
        if cx:
            v = pltpu.roll(v, 1 if cx > 0 else 127, 1)
        return v

    def stream_inside(z, _):
        bits = B[rows_of(z), :]
        pore = (bits & 1) != 0
        here = [F[d, z + 1] for d in range(19)]
        out_pop[0, rows_of(z), :] = here[0]
        for d in range(1, 19):
            cz = FLOW_DIRS[d][2]
            v = shift_in_plane(d, F[d, z + (1 - cz)] if cz else here[d])
            out_pop[d, rows_of(z), :] = jnp.where(
                (bits & (1 << d)) != 0, v, jnp.where(pore, here[OPP[d]], here[d]))
        return 0

    def edges_yz(slot):
        for si, s in enumerate(SIGNS):
            z = 0 if s > 0 else size_z - 1
            bits = B[rows_of(z), :]
            for j, d in enumerate(Z_SIDE[si]):
                v = shift_in_plane(d, ZH[slot, si, j])
                out_pop[d, rows_of(z), :] = jnp.where((bits & (1 << d)) != 0, v, out_pop[d, rows_of(z), :])
        for si, s in enumerate(SIGNS):
            at = pl.ds(0 if s > 0 else 15, size_z, stride=16)
            bits = B[at, :]
            for j, d in enumerate(Y_SIDE[si]):
                cx = FLOW_DIRS[d][0]
                v = YH[slot, si, j] if j < 3 else YC[si, j - 3]
                if cx:
                    v = pltpu.roll(v, 1 if cx > 0 else 127, 1)
                out_pop[d, at, :] = jnp.where((bits & (1 << d)) != 0, v, out_pop[d, at, :])

    def edge_x(z):
        bits = B[rows_of(z), :]
        p = [out_pop[d, rows_of(z), :] for d in range(19)]
        for si, s in enumerate(SIGNS):
            edge = jnp.where(lane == (0 if s > 0 else 127), bits, 0)
            for j, d in enumerate(X_SIDE[si]):
                back = (128 if s > 0 else 127) - 16 * j - z
                if s > 0 and j == 0:
                    back = lax.rem(back, 128)
                p[d] = jnp.where((edge & (1 << d)) != 0, pltpu.roll(XC[si], back, 1), p[d])
                out_pop[d, rows_of(z), :] = p[d]
        return p, bits

    def edge_x_collide(z, acc):
        p, bits = edge_x(z)
        moments(z, p, jnp.where((bits & 1) != 0, 1.0, 0.0))
        return collide_solute(z, acc)

    def solute_post(body):
        SM[0, 0], SM[0, 1] = planes_loop(size_z, body, zero2)
        for si in range(2):
            SM[2, si] = S[5 + si, size_z if si == 0 else 1]

    def step(t, last):
        slot = lax.rem(t + 1, 2)
        start, finish = exchange(solute_messages(), s_send, lambda k: s_recv.at[k])
        start(lambda off: True)
        finish()
        S[5, 0] = SH[2, 0]
        S[6, size_z + 1] = SH[2, 1]

        def collide(z, acc):
            return collide_flow(z, acc, stream_solute(z, None))

        XM[0], XM[1] = planes_loop(size_z, collide, zero2)
        z_pack()
        start, finish = exchange(flow_messages(slot), f_send, lambda k: f_recv.at[slot, k])
        start(z_face)
        start(not_z_face)
        if last:
            lax.fori_loop(0, comps, unplace, 0)
            for copy in back:
                copy.start()
        planes_loop(size_z, stream_inside, 0)
        finish()
        flow_halo(slot)
        edges_yz(slot)
        if last:
            planes_loop(size_z, lambda z, _: (edge_x(z), 0)[1], 0)
        else:
            solute_post(edge_x_collide)

    solute_post(collide_solute)
    lax.fori_loop(0, STEPS - 1, lambda t, _: (step(t, False), 0)[1], 0)
    step(jnp.int32(STEPS - 1), True)
    store_pop = pltpu.make_async_copy(out_pop, pop_out, io_sem.at[5])
    store_pop.start()

    for copy in back:
        copy.wait()

    def deliver(c, _):
        for s in range(slots):
            T[c, s * rows:(s + 1) * rows, :] = choose(slot_where[s], pairs_of(recv2, c))
        for r in range(rows):
            out_sol[c, :, r * 128:(r + 1) * 128] = T[c, pl.ds(r, slots, stride=rows), :]
        pltpu.make_async_copy(out_sol.at[c], sol_out.at[c], sol_sem.at[c]).start()
        return 0

    lax.fori_loop(0, comps, deliver, 0)
    for c in range(comps):
        pltpu.make_async_copy(out_sol.at[c], sol_out.at[c], sol_sem.at[c]).wait()
    store_pop.wait()


def shards(sizes, populations, solute_state, pore_mask, block_slot, slot_block):
    n_z = sizes[2]
    tiles = block_slot.shape[2]
    cap = -(-tiles // n_z)
    comps, slots, cells = solute_state.shape
    rows = cells // 128
    sz, sy, sx = pore_mask.shape
    f32 = jnp.float32
    blocks = pltpu.VMEM((n_z, cap, comps, rows, 128), f32)
    dma = pltpu.SemaphoreType.DMA
    hbm = pl.BlockSpec(memory_space=pl.ANY)
    new_populations, new_solute = pl.pallas_call(
        functools.partial(kernel, sizes, cap),
        out_shape=(
            jax.ShapeDtypeStruct((19, sz * sy, sx), f32),
            jax.ShapeDtypeStruct(solute_state.shape, f32),
        ),
        in_specs=[hbm] * 5,
        out_specs=(hbm, hbm),
        scratch_shapes=[
            pltpu.VMEM((19, sz * sy, sx), f32),
            pltpu.VMEM(solute_state.shape, f32),
            pltpu.VMEM(solute_state.shape, f32),
            pltpu.VMEM((sz * sy, sx), jnp.int32),
            pltpu.SMEM(block_slot.shape, jnp.int32),
            pltpu.SMEM(slot_block.shape, jnp.int32),
            pltpu.VMEM((19, sz + 2, sy, sx), f32),
            pltpu.VMEM((7, sz, sy, sx), f32),
            pltpu.VMEM((7, sz + 2, sy, sx), f32),
            pltpu.VMEM((4, sz, sy, sx), f32),
            pltpu.VMEM((sz * sy, sx), jnp.int32),
            pltpu.VMEM((2, 16, 128), f32),
            pltpu.VMEM((2, 5, 16, 128), f32),
            pltpu.VMEM((2, 5, 16, 128), f32),
            pltpu.VMEM((2, 2, 5, 16, 128), f32),
            pltpu.VMEM((2, 2, 5, 16, 128), f32),
            pltpu.VMEM((2, 2, 2, 8, 128), f32),
            pltpu.VMEM((2, 2, 5, 16, 128), f32),
            pltpu.VMEM((2, 16, 128), f32),
            pltpu.VMEM((2, 2, 16, 128), f32),
            pltpu.VMEM((3, 2, 16, 128), f32),
            pltpu.VMEM((3, 2, 16, 128), f32),
            pltpu.VMEM((comps, slots * rows, 128), f32),
            blocks, blocks, blocks, blocks,
            dma((18,)), dma((2, 18)), dma((6,)), dma((6,)),
            dma((n_z,)), dma((n_z,)), dma((n_z,)), dma((n_z,)), dma((2,)), dma((6,)), dma((comps,)),
        ],
        compiler_params=pltpu.CompilerParams(
            collective_id=0, has_side_effects=True, vmem_limit_bytes=56 * 1024 * 1024),
    )(populations.reshape(19, sz * sy, sx), solute_state, pore_mask.reshape(sz * sy, sx), block_slot, slot_block)
    return new_populations.reshape(populations.shape), new_solute


def solution(mesh):
    sizes = tuple(mesh.shape[a] for a in AXES)
    in_specs = (
        P(None, "gz", "gy", "gx"),
        P(None, ("gx", "gy", "gz"), None),
        P("gz", "gy", "gx"),
        P("gz", "gy", "gx"),
        P(("gx", "gy", "gz")),
    )
    out_specs = (P(None, "gz", "gy", "gx"), P(None, ("gx", "gy", "gz"), None))
    return jax.shard_map(
        functools.partial(shards, sizes), mesh=mesh, in_specs=in_specs, out_specs=out_specs, check_vma=False)
```
